32 devices in a mesh: partner: 8 (over y, x, core), blk: 4 (over z).
Axes of the slice: x: 2, y: 2, z: 4, core: 2. Of those that a mesh axis runs over, the one named last changes fastest.
Arguments:
- tensor_slab: float32 [8, 8192, 2048], P(None, 'partner', 'blk'), may hold values from -6 to 6
- sign_flips: int32 [8192], P('partner'), may hold values from -1 to 1, as said below
- mode2_factor: float32 [2048, 64], P('blk'), may hold values from -6 to 6
- mode3_factor: float32 [8, 64], replicated, may hold values from -6 to 6
- fibre_col: int32 [2048], P('blk'), may hold values from 0 to 511
- fibre_depth: int32 [2048], P('blk'), may hold values from 0 to 7
Outputs:
- mixed_slab: float32 [8, 8192, 2048], P(None, 'partner', 'blk')
- factor_update: float32 [8192, 64], P('partner')
The draws below stay inside these ranges and needn't reach their ends.
Inputs may be any that keep to these rules, and one draw needn't show every extreme that they name: `sign_flips`: every entry is -1 or 1.
All inputs are finite; a program needn't handle non-finite values.
Results may differ from the reference program's by a relative error of at most 0.000098.
Values sent between devices are 32-bit elements; how exact they have to be, the bound alone decides.
A program may use at most 128 MiB of HBM per device.

```python
import math
import jax
import jax.numpy as jnp
from jax import lax

I = 8192
R = 64
K = 8
JB = 512
S_DEV = 512
J = 2048
TOTAL = 2048


def draw_sign_flips(key, part):
    key = jax.random.fold_in(key, 7)
    return (2 * jax.random.randint(key, (I,), 0, 2) - 1).astype(jnp.int32)


def with_ends(values, own_key, least, top_value):
    place = [jax.random.randint(jax.random.fold_in(own_key, axis), (), 0, length) for axis, length in enumerate(values.shape)]
    widest = values.shape.index(max(values.shape))
    beside = place[:widest] + [(place[widest] + 1) % values.shape[widest]] + place[widest + 1:]
    return values.at[tuple(place)].set(least).at[tuple(beside)].set(top_value)


def block_levels(rng, dims, shards, least, top_value):
    loudness, own = 1.0, jax.random.fold_in(rng, 6)
    for axis_at, parts in shards:
        steps = jnp.exp(jax.random.uniform(jax.random.fold_in(own, axis_at), (parts,), jnp.float32, least / len(shards), top_value / len(shards)))
        loudness = loudness * jnp.repeat(steps, dims[axis_at] // parts).reshape([-1 if axis == axis_at else 1 for axis in range(len(dims))])
    return loudness


def normal_values(own_key, shape, spread, reach, pieces=(), held_as=jnp.bfloat16):
    values = spread * jax.random.normal(own_key, shape, jnp.float32)
    if pieces:
        values = values * block_levels(own_key, shape, pieces, -0.22, 0.18)
    return jnp.clip(values, -reach, reach).astype(held_as)


def setup_inputs(seed: int = 0) -> dict:
    key_list = jax.random.split(jax.random.key(seed), 7)
    tensor_slab = normal_values(key_list[0], (K, I, J), 1.0, 6.0, ((1, 8), (2, 4)), jnp.float32)
    sign_flips = draw_sign_flips(jax.random.fold_in(key_list[6], 71), 0)
    mode2_factor = normal_values(key_list[2], (J, R), 1.0, 6.0, ((0, 4),), jnp.float32)
    mode3_factor = normal_values(key_list[3], (K, R), 1.0, 6.0, (), jnp.float32)
    fibre_col = with_ends(jax.random.randint(key_list[4], (TOTAL,), 0, JB), jax.random.fold_in(key_list[4], 1), 0, JB - 1).astype(jnp.int32)
    fibre_depth = with_ends(jax.random.randint(key_list[5], (TOTAL,), 0, K), jax.random.fold_in(key_list[5], 1), 0, K - 1).astype(jnp.int32)
    return {"tensor_slab": tensor_slab, "sign_flips": sign_flips, "mode2_factor": mode2_factor, "mode3_factor": mode3_factor, "fibre_col": fibre_col, "fibre_depth": fibre_depth}


ridge = 0.1

def walsh_rows(field):
    depth_count, length_all, column_count = field.shape
    stride_len = 1
    while stride_len < length_all:
        shaped = field.reshape(depth_count, length_all // (2 * stride_len), 2, stride_len, column_count)
        upper_part = shaped[:, :, 0]
        lower_part = shaped[:, :, 1]
        field = jnp.stack([upper_part + lower_part, upper_part - lower_part], axis=2).reshape(depth_count, length_all, column_count)
        stride_len = stride_len * 2
    return field

def reference(tensor_slab, sign_flips, mode2_factor, mode3_factor, fibre_col, fibre_depth):
    flipped = tensor_slab * sign_flips.astype(jnp.float32)[None, :, None]
    mixed_slab = walsh_rows(flipped) * (1.0 / math.sqrt(I))
    block_of = (jnp.arange(TOTAL, dtype=jnp.int32) // S_DEV).astype(jnp.int32)
    global_col = (fibre_col + block_of * JB).astype(jnp.int32)
    picked = mixed_slab[fibre_depth, :, global_col]
    khatri = mode2_factor[global_col] * mode3_factor[fibre_depth]
    moment = lax.dot_general(picked, khatri, (((0,), (0,)), ((), ())), precision=lax.Precision.HIGHEST) * (1.0 / math.sqrt(TOTAL))
    gram = lax.dot_general(khatri, khatri, (((0,), (0,)), ((), ())), precision=lax.Precision.HIGHEST) * (1.0 / TOTAL)
    gram = gram + ridge * jnp.eye(R, dtype=jnp.float32)
    factor_update = jnp.linalg.solve(gram, moment.T).T
    return (mixed_slab, factor_update)
```

```python
import functools
import math

import jax
import jax.numpy as jnp
from jax import lax
from jax.experimental import pallas as pl
from jax.experimental.pallas import tpu as pltpu
from jax.sharding import PartitionSpec as P

ridge = 0.1
MESH = pl.DeviceIdType.MESH
f32 = jnp.float32
bf16 = jnp.bfloat16


def solve_normal(gram, moment):
    factor_chol = jnp.linalg.cholesky(gram)
    return jax.scipy.linalg.cho_solve((factor_chol, True), moment.T).T


def contract_samples(picked, khatri):
    return lax.dot_general(
        picked, khatri, (((0,), (0,)), ((), ())), precision=lax.Precision.HIGHEST
    )


def walsh_tile(order):
    rows_idx = lax.broadcasted_iota(jnp.int32, (order, order), 0)
    cols_idx = lax.broadcasted_iota(jnp.int32, (order, order), 1)
    parity = jnp.bitwise_and(rows_idx, cols_idx)
    shift = order.bit_length() - 1
    while shift > 1:
        shift = (shift + 1) // 2
        parity = jnp.bitwise_xor(parity, jnp.right_shift(parity, shift))
    return (1 - 2 * jnp.bitwise_and(parity, 1)).astype(f32)


def butterflies(parts):
    stride = 1
    while stride < len(parts):
        parts = [
            parts[at] + parts[at + stride] if at & stride == 0 else parts[at - stride] - parts[at]
            for at in range(len(parts))
        ]
        stride *= 2
    return parts


def split_two(value):
    high = value.astype(bf16)
    return high, (value - high.astype(f32)).astype(bf16)


def mixing_kernel(plan, slab, signs, out, held, landed, core_landed, near_signs, tables,
                  load_sem, link_send, link_recv, core_send, core_recv, sign_send, sign_recv, out_sem):
    parties, links, per_group, depth, slots = plan
    slices, rows, cols = held.shape
    tile = tables.shape[-1]
    blocks = rows // tile
    me = lax.axis_index("partner")

    def peer(bit):
        return jnp.bitwise_xor(me, 1 << bit)

    def side(bit):
        return (1 - 2 * jnp.bitwise_and(jnp.right_shift(me, bit), 1)).astype(f32)

    barrier = pltpu.get_barrier_semaphore()
    for bit in range(links + 1):
        pl.semaphore_signal(barrier, inc=1, device_id={"partner": peer(bit)}, device_id_type=MESH)
    pl.semaphore_wait(barrier, links + 1)

    total = links * per_group

    def chunk_at(link, slot):
        phase, turn = divmod(slot, per_group)
        chunk = (link - phase) % links + links * turn
        return chunk if chunk < slices else None

    def link_copy(link, slot):
        chunk = chunk_at(link, slot)
        if chunk is None:
            return None
        source = slab if slot < per_group else held
        return pltpu.make_async_remote_copy(
            src_ref=source.at[chunk],
            dst_ref=landed.at[link, slot % slots],
            send_sem=link_send.at[link, slot % slots],
            recv_sem=link_recv.at[link, slot % slots],
            device_id={"partner": peer(link + 1)},
            device_id_type=MESH,
        )

    def core_copy(link, slot):
        chunk = chunk_at(link, slot)
        if chunk is None:
            return None
        return pltpu.make_async_remote_copy(
            src_ref=held.at[chunk],
            dst_ref=core_landed.at[link, slot % 2],
            send_sem=core_send.at[link, slot % 2],
            recv_sem=core_recv.at[link, slot % 2],
            device_id={"partner": peer(0)},
            device_id_type=MESH,
        )

    def sign_copy(link):
        return pltpu.make_async_remote_copy(
            src_ref=signs,
            dst_ref=near_signs.at[link],
            send_sem=sign_send.at[link],
            recv_sem=sign_recv.at[link],
            device_id={"partner": peer(link + 1)},
            device_id_type=MESH,
        )

    def load_copy(chunk):
        return pltpu.make_async_copy(slab.at[chunk], held.at[chunk], load_sem.at[chunk])

    def out_copy(chunk):
        return pltpu.make_async_copy(held.at[chunk], out.at[chunk], out_sem.at[chunk])

    def combine(chunk, other, bit, scale):
        mine = side(bit) * scale
        step = min(rows, 64)

        @pl.loop(0, rows // step)
        def _(at):
            span = pl.ds(pl.multiple_of(at * step, step), step)
            held[chunk, span, :] = held[chunk, span, :] * mine + other[span, :] * scale

    for link in range(links):
        sign_copy(link).start()
    for slot in range(depth):
        for link in range(links):
            copy = link_copy(link, slot)
            if copy is not None:
                copy.start()
    for chunk in range(slices):
        load_copy(chunk).start()

    for link in range(links):
        sign_copy(link).wait()
    own_table = walsh_tile(tile)
    for link in range(links):
        for block in range(blocks):
            span = slice(block * tile, (block + 1) * tile)
            tables[link, 0, block] = (own_table * (signs[0:1, span] * side(link + 1))).astype(bf16)
            tables[link, 1, block] = (own_table * near_signs[link, 0:1, span]).astype(bf16)
    for chunk in range(slices):
        load_copy(chunk).wait()

    def transform(slot):
        count = min(links, slices - links * slot)
        width = min(cols, 256)
        tiles = cols // width

        @pl.loop(0, count * tiles)
        def _(at):
            link = at // tiles
            span = pl.ds(pl.multiple_of((at % tiles) * width, width), width)
            chunk = link + links * slot
            parts = []
            for block in range(blocks):
                lines = slice(block * tile, (block + 1) * tile)
                own_high, own_low = split_two(held[chunk, lines, span])
                far_high, far_low = split_two(landed[link, slot % slots, lines, span])
                own, far = tables[link, 0, block], tables[link, 1, block]
                sums = jnp.dot(own, own_high, preferred_element_type=f32)
                sums += jnp.dot(own, own_low, preferred_element_type=f32)
                sums += jnp.dot(far, far_high, preferred_element_type=f32)
                sums += jnp.dot(far, far_low, preferred_element_type=f32)
                parts.append(sums)
            for block, part in enumerate(butterflies(parts)):
                held[chunk, block * tile:(block + 1) * tile, span] = part

    scale = 1.0 / math.sqrt(rows * parties)
    for slot in range(total):
        if 1 <= slot <= per_group:
            for link in range(links):
                copy = core_copy(link, slot - 1)
                if copy is not None:
                    copy.wait()
                    combine(chunk_at(link, slot - 1), core_landed.at[link, (slot - 1) % 2], 0, 1.0)
        if slot < per_group:
            for link in range(links):
                copy = link_copy(link, slot)
                if copy is not None:
                    copy.wait()
            transform(slot)
            for link in range(links):
                copy = core_copy(link, slot)
                if copy is not None:
                    copy.start()
        else:
            last = slot >= total - per_group
            for link in range(links):
                copy = link_copy(link, slot)
                if copy is not None:
                    copy.wait()
                    chunk = chunk_at(link, slot)
                    combine(chunk, landed.at[link, slot % slots], link + 1, scale if last else 1.0)
                    if last:
                        out_copy(chunk).start()
        if slot + depth < total:
            for link in range(links):
                copy = link_copy(link, slot + depth)
                if copy is not None:
                    copy.start()
    for chunk in range(slices):
        out_copy(chunk).wait()


def mix(slab, sign_flips):
    slices, rows, cols = slab.shape
    parties = lax.axis_size("partner")
    links = parties.bit_length() - 2
    per_group = -(-slices // links)
    depth = 2
    total = links * per_group
    slots = 4 if slices % links == 0 else total
    tile = min(256, rows)
    blocks = rows // tile
    signs = jnp.broadcast_to(sign_flips.astype(f32)[None, :], (8, rows))
    plan = (parties, links, per_group, depth, slots)
    return pl.pallas_call(
        functools.partial(mixing_kernel, plan),
        out_shape=jax.ShapeDtypeStruct(slab.shape, f32),
        in_specs=[
            pl.BlockSpec(memory_space=pl.ANY),
            pl.BlockSpec(memory_space=pltpu.VMEM),
        ],
        out_specs=pl.BlockSpec(memory_space=pl.ANY),
        scratch_shapes=[
            pltpu.VMEM((slices, rows, cols), f32),
            pltpu.VMEM((links, slots, rows, cols), f32),
            pltpu.VMEM((links, 2, rows, cols), f32),
            pltpu.VMEM((links, 8, rows), f32),
            pltpu.VMEM((links, 2, blocks, tile, tile), bf16),
            pltpu.SemaphoreType.DMA((slices,)),
            pltpu.SemaphoreType.DMA((links, slots)),
            pltpu.SemaphoreType.DMA((links, slots)),
            pltpu.SemaphoreType.DMA((links, 2)),
            pltpu.SemaphoreType.DMA((links, 2)),
            pltpu.SemaphoreType.DMA((links,)),
            pltpu.SemaphoreType.DMA((links,)),
            pltpu.SemaphoreType.DMA((slices,)),
        ],
        compiler_params=pltpu.CompilerParams(
            collective_id=0, has_side_effects=True, vmem_limit_bytes=56 * 2**20
        ),
    )(slab, signs)


def shards(tensor_slab, sign_flips, mode2_factor, mode3_factor, fibre_col, fibre_depth):
    mixed_slab = mix(tensor_slab, sign_flips)
    total_count = fibre_col.shape[0] * lax.axis_size("blk")
    picked = mixed_slab[fibre_depth, :, fibre_col]
    khatri = mode2_factor[fibre_col] * mode3_factor[fibre_depth]
    moment_scale = 1.0 / math.sqrt(total_count)
    gram_part = contract_samples(khatri, khatri) * (1.0 / total_count)
    identity = jnp.eye(khatri.shape[1], dtype=jnp.float32)
    moment_part = contract_samples(picked, khatri) * moment_scale
    moment, gram = lax.psum((moment_part, gram_part), "blk")
    factor_update = solve_normal(gram + ridge * identity, moment)
    return (mixed_slab, factor_update)


def solution(mesh):
    return jax.shard_map(
        shards,
        mesh=mesh,
        in_specs=(P(None, "partner", "blk"), P("partner"), P("blk", None), P(), P("blk"), P("blk")),
        out_specs=(P(None, "partner", "blk"), P("partner", None)),
        check_vma=False,
    )
```

```python
import functools
import math

import jax
import jax.numpy as jnp
from jax import lax
from jax.experimental import pallas as pl
from jax.experimental.pallas import tpu as pltpu
from jax.sharding import PartitionSpec as P

ridge = 0.1
MESH = pl.DeviceIdType.MESH
f32 = jnp.float32
bf16 = jnp.bfloat16


def walsh_tile(order):
    rows_idx = lax.broadcasted_iota(jnp.int32, (order, order), 0)
    cols_idx = lax.broadcasted_iota(jnp.int32, (order, order), 1)
    parity = jnp.bitwise_and(rows_idx, cols_idx)
    shift = order.bit_length() - 1
    while shift > 1:
        shift = (shift + 1) // 2
        parity = jnp.bitwise_xor(parity, jnp.right_shift(parity, shift))
    return (1 - 2 * jnp.bitwise_and(parity, 1)).astype(f32)


def butterflies(parts):
    stride = 1
    while stride < len(parts):
        parts = [
            parts[at] + parts[at + stride] if at & stride == 0 else parts[at - stride] - parts[at]
            for at in range(len(parts))
        ]
        stride *= 2
    return parts


def split_two(value):
    high = value.astype(bf16)
    return high, (value - high.astype(f32)).astype(bf16)


def exact_dot(left, right):
    return jnp.dot(left, right, precision=lax.Precision.HIGHEST, preferred_element_type=f32)


def inverse_of(gram):
    order = gram.shape[0]
    rows_idx = lax.broadcasted_iota(jnp.int32, (order, order), 0)
    cols_idx = lax.broadcasted_iota(jnp.int32, (order, order), 1)

    def eliminate(at, work):
        on_row, on_col = rows_idx == at, cols_idx == at
        row = jnp.sum(jnp.where(on_row, work, 0.0), axis=0, keepdims=True)
        col = jnp.sum(jnp.where(on_col, work, 0.0), axis=1, keepdims=True)
        pivot = jnp.sum(jnp.where(on_col[0:1], row, 0.0), axis=1, keepdims=True)
        row = jnp.where(on_col[0:1], 1.0, row) / pivot
        return jnp.where(on_row, row, jnp.where(on_col, 0.0, work) - col * row)

    found = lax.fori_loop(0, order, eliminate, gram)
    identity = (rows_idx == cols_idx).astype(f32)
    return found + exact_dot(found, identity - exact_dot(gram, found))


def mixing_kernel(plan, slab, flips, fibre_col, fibre_depth, mode2_wide, mode3, out, update_wide,
                  held, landed, core_landed, signs, near_signs, tables,
                  mode2, update, moment, gram, moment_in, gram_in, packed, packed_in, gathered,
                  load_sem, link_send, link_recv, core_send, core_recv, sign_send, sign_recv, out_sem,
                  moment_send, moment_recv, gram_send, gram_recv, pack_send, pack_recv, gather_send, gather_recv):
    parties, blks, links, per_group, depth, slots = plan
    slices, rows, cols = held.shape
    tile = tables.shape[-1]
    blocks = rows // tile
    me = lax.axis_index("partner")
    my_blk = lax.axis_index("blk")
    share = rows // blks
    rank = mode2.shape[1]
    scale = 1.0 / math.sqrt(rows * parties)
    sample_count = fibre_col.shape[1] * blks

    def peer(bit):
        return jnp.bitwise_xor(me, 1 << bit)

    def side(bit):
        return (1 - 2 * jnp.bitwise_and(jnp.right_shift(me, bit), 1)).astype(f32)

    barrier = pltpu.get_barrier_semaphore()
    for bit in range(links + 1):
        pl.semaphore_signal(barrier, inc=1, device_id={"partner": peer(bit)}, device_id_type=MESH)
    for off in range(1, blks):
        pl.semaphore_signal(barrier, inc=1, device_id={"blk": lax.rem(my_blk + off, blks)}, device_id_type=MESH)
    pl.semaphore_wait(barrier, links + blks)

    total = links * per_group

    def chunk_at(link, slot):
        phase, turn = divmod(slot, per_group)
        chunk = (link - phase) % links + links * turn
        return chunk if chunk < slices else None

    def link_copy(link, slot):
        chunk = chunk_at(link, slot)
        if chunk is None:
            return None
        source = slab if slot < per_group else held
        return pltpu.make_async_remote_copy(
            src_ref=source.at[chunk],
            dst_ref=landed.at[link, slot % slots],
            send_sem=link_send.at[link, slot % slots],
            recv_sem=link_recv.at[link, slot % slots],
            device_id={"partner": peer(link + 1)},
            device_id_type=MESH,
        )

    def core_copy(link, slot):
        chunk = chunk_at(link, slot)
        if chunk is None:
            return None
        return pltpu.make_async_remote_copy(
            src_ref=held.at[chunk],
            dst_ref=core_landed.at[link, slot % 2],
            send_sem=core_send.at[link, slot % 2],
            recv_sem=core_recv.at[link, slot % 2],
            device_id={"partner": peer(0)},
            device_id_type=MESH,
        )

    def sign_copy(link):
        return pltpu.make_async_remote_copy(
            src_ref=signs,
            dst_ref=near_signs.at[link],
            send_sem=sign_send.at[link],
            recv_sem=sign_recv.at[link],
            device_id={"partner": peer(link + 1)},
            device_id_type=MESH,
        )

    def load_copy(chunk):
        return pltpu.make_async_copy(slab.at[chunk], held.at[chunk], load_sem.at[chunk])

    def out_copy(chunk):
        return pltpu.make_async_copy(held.at[chunk], out.at[chunk], out_sem.at[chunk])

    def combine(chunk, other, bit, scale):
        mine = side(bit) * scale
        step = min(rows, 64)

        @pl.loop(0, rows // step)
        def _(at):
            span = pl.ds(pl.multiple_of(at * step, step), step)
            held[chunk, span, :] = held[chunk, span, :] * mine + other[span, :] * scale

    for slot in range(depth):
        for link in range(links):
            copy = link_copy(link, slot)
            if copy is not None:
                copy.start()
    for chunk in range(slices):
        load_copy(chunk).start()
    signs[...] = jnp.broadcast_to(flips[...].astype(f32), signs.shape)
    for link in range(links):
        sign_copy(link).start()

    for link in range(links):
        sign_copy(link).wait()
    own_table = walsh_tile(tile)
    for link in range(links):
        for block in range(blocks):
            span = slice(block * tile, (block + 1) * tile)
            tables[link, 0, block] = (own_table * (signs[0:1, span] * side(link + 1))).astype(bf16)
            tables[link, 1, block] = (own_table * near_signs[link, 0:1, span]).astype(bf16)
    for chunk in range(slices):
        load_copy(chunk).wait()

    def transform(slot):
        count = min(links, slices - links * slot)
        width = min(cols, 256)
        tiles = cols // width

        @pl.loop(0, count * tiles)
        def _(at):
            link = at // tiles
            span = pl.ds(pl.multiple_of((at % tiles) * width, width), width)
            chunk = link + links * slot
            parts = []
            for block in range(blocks):
                lines = slice(block * tile, (block + 1) * tile)
                own_high, own_low = split_two(held[chunk, lines, span])
                far_high, far_low = split_two(landed[link, slot % slots, lines, span])
                own, far = tables[link, 0, block], tables[link, 1, block]
                sums = jnp.dot(own, own_high, preferred_element_type=f32)
                sums += jnp.dot(own, own_low, preferred_element_type=f32)
                sums += jnp.dot(far, far_high, preferred_element_type=f32)
                sums += jnp.dot(far, far_low, preferred_element_type=f32)
                parts.append(sums)
            for block, part in enumerate(butterflies(parts)):
                held[chunk, block * tile:(block + 1) * tile, span] = part

    def rows_of(blk):
        return pl.ds(pl.multiple_of(blk * share, share), share)

    def moment_copy(off):
        target = lax.rem(my_blk + off, blks)
        return pltpu.make_async_remote_copy(
            src_ref=moment.at[rows_of(target)],
            dst_ref=moment_in.at[off - 1],
            send_sem=moment_send.at[off - 1],
            recv_sem=moment_recv.at[off - 1],
            device_id={"blk": target},
            device_id_type=MESH,
        )

    def gram_copy(off):
        return pltpu.make_async_remote_copy(
            src_ref=gram,
            dst_ref=gram_in.at[off - 1],
            send_sem=gram_send.at[off - 1],
            recv_sem=gram_recv.at[off - 1],
            device_id={"blk": lax.rem(my_blk + off, blks)},
            device_id_type=MESH,
        )

    def pack_copy(bit):
        return pltpu.make_async_remote_copy(
            src_ref=packed.at[bit],
            dst_ref=packed_in.at[bit],
            send_sem=pack_send.at[bit],
            recv_sem=pack_recv.at[bit],
            device_id={"partner": peer(bit)},
            device_id_type=MESH,
        )

    def gather_copy(off):
        return pltpu.make_async_remote_copy(
            src_ref=packed.at[links + 1],
            dst_ref=gathered.at[off - 1],
            send_sem=gather_send.at[off - 1],
            recv_sem=gather_recv.at[off - 1],
            device_id={"blk": lax.rem(my_blk + off, blks)},
            device_id_type=MESH,
        )

    def contract_local():
        mode2[...] = mode2_wide[...].T
        moment[...] = jnp.zeros_like(moment)
        gram[...] = jnp.zeros_like(gram)
        samples = fibre_col.shape[1]

        @pl.loop(0, slices)
        def _(chunk):
            place = lax.broadcasted_iota(jnp.int32, (cols, samples), 0) + chunk * cols
            sampled = fibre_depth[...] * cols + fibre_col[...]
            counts = jnp.sum((place == sampled).astype(f32), axis=1, keepdims=True)
            khatri = mode2[...] * mode3[pl.ds(chunk, 1), :]
            weights = khatri * counts
            gram[...] += exact_dot(weights.T, khatri)

            @pl.loop(0, blocks)
            def _(block):
                lines = pl.ds(pl.multiple_of(block * tile, tile), tile)
                moment[lines, :] += exact_dot(held[chunk, lines, :], weights)

        parts = []
        for block in range(blocks):
            value = moment[block * tile:(block + 1) * tile, :]
            high, rest = split_two(value)
            low = (value - high.astype(f32) - rest.astype(f32)).astype(bf16)
            table = tables[0, 0, block]
            sums = jnp.dot(table, low, preferred_element_type=f32)
            sums += jnp.dot(table, rest, preferred_element_type=f32)
            sums += jnp.dot(table, high, preferred_element_type=f32)
            parts.append(sums * side(1))
        for block, part in enumerate(butterflies(parts)):
            moment[block * tile:(block + 1) * tile, :] = part
        for off in range(1, blks):
            moment_copy(off).start()
            gram_copy(off).start()

    def solve_share():
        for off in range(1, blks):
            moment_copy(off).wait()
            gram_copy(off).wait()
        whole_gram = gram[...]
        own = moment[rows_of(my_blk), :]
        for off in range(1, blks):
            whole_gram = whole_gram + gram_in[off - 1]
            own = own + moment_in[off - 1]
        rows_idx = lax.broadcasted_iota(jnp.int32, (rank, rank), 0)
        cols_idx = lax.broadcasted_iota(jnp.int32, (rank, rank), 1)
        whole_gram = whole_gram * (1.0 / sample_count) + jnp.where(rows_idx == cols_idx, ridge, 0.0)
        solved = exact_dot(own * (scale / math.sqrt(sample_count)), inverse_of(whole_gram))
        packed[0] = jnp.concatenate([solved[: share // 2], solved[share // 2:]], axis=1)
        pack_copy(0).start()

    def pack_step(bit):
        pack_copy(bit).wait()
        packed[bit + 1] = packed[bit] * side(bit) + packed_in[bit]
        if bit < links:
            pack_copy(bit + 1).start()
        else:
            for off in range(1, blks):
                gather_copy(off).start()

    def write_share(blk, value):
        half = share // 2
        for at in range(2):
            lines = pl.ds(pl.multiple_of(blk * share + at * half, half), half)
            update[lines, :] = value[:, at * rank:(at + 1) * rank]

    def write_update():
        write_share(my_blk, packed[links + 1])
        for off in range(1, blks):
            gather_copy(off).wait()
            write_share(lax.rem(my_blk + blks - off, blks), gathered[off - 1])
        update_wide[...] = update[...].T

    contract_local()
    for slot in range(total):
        if 1 <= slot <= per_group:
            for link in range(links):
                copy = core_copy(link, slot - 1)
                if copy is not None:
                    copy.wait()
                    combine(chunk_at(link, slot - 1), core_landed.at[link, (slot - 1) % 2], 0, 1.0)
        if slot < per_group:
            for link in range(links):
                copy = link_copy(link, slot)
                if copy is not None:
                    copy.wait()
            transform(slot)
            for link in range(links):
                copy = core_copy(link, slot)
                if copy is not None:
                    copy.start()
        else:
            last = slot >= total - per_group
            for link in range(links):
                copy = link_copy(link, slot)
                if copy is not None:
                    copy.wait()
                    chunk = chunk_at(link, slot)
                    combine(chunk, landed.at[link, slot % slots], link + 1, scale if last else 1.0)
                    if last:
                        out_copy(chunk).start()
        if slot + depth < total:
            for link in range(links):
                copy = link_copy(link, slot + depth)
                if copy is not None:
                    copy.start()
        if slot == 1:
            solve_share()
        elif 2 <= slot <= links + 2:
            pack_step(slot - 2)
        elif slot == links + 3:
            write_update()
    for chunk in range(slices):
        out_copy(chunk).wait()


def shards(tensor_slab, sign_flips, mode2_factor, mode3_factor, fibre_col, fibre_depth):
    slices, rows, cols = tensor_slab.shape
    rank = mode2_factor.shape[1]
    parties, blks = lax.axis_size("partner"), lax.axis_size("blk")
    links = parties.bit_length() - 2
    per_group = -(-slices // links)
    depth = 2
    total = links * per_group
    slots = 4 if slices % links == 0 else total
    tile = min(256, rows)
    blocks = rows // tile
    share = rows // blks
    packed_shape = (share // 2, 2 * rank)
    others = max(blks - 1, 1)
    plan = (parties, blks, links, per_group, depth, slots)
    dma = pltpu.SemaphoreType.DMA
    vmem = pl.BlockSpec(memory_space=pltpu.VMEM)
    anywhere = pl.BlockSpec(memory_space=pl.ANY)
    mixed_slab, update_wide = pl.pallas_call(
        functools.partial(mixing_kernel, plan),
        out_shape=(
            jax.ShapeDtypeStruct(tensor_slab.shape, f32),
            jax.ShapeDtypeStruct((rank, rows), f32),
        ),
        in_specs=[anywhere, vmem, vmem, vmem, vmem, vmem],
        out_specs=(anywhere, vmem),
        scratch_shapes=[
            pltpu.VMEM((slices, rows, cols), f32),
            pltpu.VMEM((links, slots, rows, cols), f32),
            pltpu.VMEM((links, 2, rows, cols), f32),
            pltpu.VMEM((8, rows), f32),
            pltpu.VMEM((links, 8, rows), f32),
            pltpu.VMEM((links, 2, blocks, tile, tile), bf16),
            pltpu.VMEM((cols, rank), f32),
            pltpu.VMEM((rows, rank), f32),
            pltpu.VMEM((rows, rank), f32),
            pltpu.VMEM((rank, rank), f32),
            pltpu.VMEM((others, share, rank), f32),
            pltpu.VMEM((others, rank, rank), f32),
            pltpu.VMEM((links + 2, *packed_shape), f32),
            pltpu.VMEM((links + 1, *packed_shape), f32),
            pltpu.VMEM((others, *packed_shape), f32),
            dma((slices,)),
            dma((links, slots)),
            dma((links, slots)),
            dma((links, 2)),
            dma((links, 2)),
            dma((links,)),
            dma((links,)),
            dma((slices,)),
            dma((others,)),
            dma((others,)),
            dma((others,)),
            dma((others,)),
            dma((links + 1,)),
            dma((links + 1,)),
            dma((others,)),
            dma((others,)),
        ],
        compiler_params=pltpu.CompilerParams(
            collective_id=0, has_side_effects=True, vmem_limit_bytes=56 * 2**20
        ),
    )(
        tensor_slab,
        sign_flips.reshape(1, rows),
        fibre_col.reshape(1, fibre_col.shape[0]),
        fibre_depth.reshape(1, fibre_depth.shape[0]),
        mode2_factor.T,
        mode3_factor,
    )
    return mixed_slab, update_wide.T


def solution(mesh):
    return jax.shard_map(
        shards,
        mesh=mesh,
        in_specs=(P(None, "partner", "blk"), P("partner"), P("blk", None), P(), P("blk"), P("blk")),
        out_specs=(P(None, "partner", "blk"), P("partner", None)),
        check_vma=False,
    )
```

```python
import functools
import math

import jax
import jax.numpy as jnp
from jax import lax
from jax.experimental import pallas as pl
from jax.experimental.pallas import tpu as pltpu
from jax.sharding import PartitionSpec as P

ridge = 0.1
MESH = pl.DeviceIdType.MESH
f32 = jnp.float32
bf16 = jnp.bfloat16


def walsh_tile(order):
    rows_idx = lax.broadcasted_iota(jnp.int32, (order, order), 0)
    cols_idx = lax.broadcasted_iota(jnp.int32, (order, order), 1)
    parity = jnp.bitwise_and(rows_idx, cols_idx)
    shift = order.bit_length() - 1
    while shift > 1:
        shift = (shift + 1) // 2
        parity = jnp.bitwise_xor(parity, jnp.right_shift(parity, shift))
    return (1 - 2 * jnp.bitwise_and(parity, 1)).astype(f32)


def butterflies(parts):
    stride = 1
    while stride < len(parts):
        parts = [
            parts[at] + parts[at + stride] if at & stride == 0 else parts[at - stride] - parts[at]
            for at in range(len(parts))
        ]
        stride *= 2
    return parts


def split_two(value):
    high = value.astype(bf16)
    return high, (value - high.astype(f32)).astype(bf16)


def exact_dot(left, right):
    return jnp.dot(left, right, precision=lax.Precision.HIGHEST, preferred_element_type=f32)


def inverse_of(gram):
    order = gram.shape[0]
    rows_idx = lax.broadcasted_iota(jnp.int32, (order, order), 0)
    cols_idx = lax.broadcasted_iota(jnp.int32, (order, order), 1)

    def eliminate(at, work):
        on_row, on_col = rows_idx == at, cols_idx == at
        row = jnp.sum(jnp.where(on_row, work, 0.0), axis=0, keepdims=True)
        col = jnp.sum(jnp.where(on_col, work, 0.0), axis=1, keepdims=True)
        pivot = jnp.sum(jnp.where(on_col[0:1], row, 0.0), axis=1, keepdims=True)
        row = jnp.where(on_col[0:1], 1.0, row) / pivot
        return jnp.where(on_row, row, jnp.where(on_col, 0.0, work) - col * row)

    found = lax.fori_loop(0, order, eliminate, gram)
    identity = (rows_idx == cols_idx).astype(f32)
    return found + exact_dot(found, identity - exact_dot(gram, found))


def split_three(value):
    high, rest = split_two(value)
    low = (value - high.astype(f32) - rest.astype(f32)).astype(bf16)
    return high, rest, low


def mixing_kernel(plan, slab, flips, fibre_col, fibre_depth, mode2_wide, mode3, out, update_wide,
                  held, landed, core_landed, signs, near_signs, tables,
                  mode2, update, moment_wide, gram_wide, moment, gram, moment_in, gram_in, packed, packed_in, gathered,
                  load_sem, link_send, link_recv, core_send, core_recv, sign_send, sign_recv, out_sem,
                  moment_send, moment_recv, gram_send, gram_recv, pack_send, pack_recv, gather_send, gather_recv):
    parties, blks, links, per_group, depth, slots = plan
    slices, rows, cols = held.shape
    tile = tables.shape[-1]
    blocks = rows // tile
    me = lax.axis_index("partner")
    my_blk = lax.axis_index("blk")
    share = rows // blks
    rank = mode2.shape[1]
    scale = 1.0 / math.sqrt(rows * parties)
    sample_count = fibre_col.shape[1] * blks

    def peer(bit):
        return jnp.bitwise_xor(me, 1 << bit)

    def side(bit):
        return (1 - 2 * jnp.bitwise_and(jnp.right_shift(me, bit), 1)).astype(f32)

    barrier = pltpu.get_barrier_semaphore()
    for bit in range(links + 1):
        pl.semaphore_signal(barrier, inc=1, device_id={"partner": peer(bit)}, device_id_type=MESH)
    for off in range(1, blks):
        pl.semaphore_signal(barrier, inc=1, device_id={"blk": lax.rem(my_blk + off, blks)}, device_id_type=MESH)
    pl.semaphore_wait(barrier, links + blks)

    total = links * per_group

    def chunk_at(link, slot):
        phase, turn = divmod(slot, per_group)
        chunk = (link - phase) % links + links * turn
        return chunk if chunk < slices else None

    def link_copy(link, slot):
        chunk = chunk_at(link, slot)
        if chunk is None:
            return None
        source = slab if slot < per_group else held
        return pltpu.make_async_remote_copy(
            src_ref=source.at[chunk],
            dst_ref=landed.at[link, slot % slots],
            send_sem=link_send.at[link, slot % slots],
            recv_sem=link_recv.at[link, slot % slots],
            device_id={"partner": peer(link + 1)},
            device_id_type=MESH,
        )

    def core_copy(link, slot):
        chunk = chunk_at(link, slot)
        if chunk is None:
            return None
        return pltpu.make_async_remote_copy(
            src_ref=held.at[chunk],
            dst_ref=core_landed.at[link, slot % 2],
            send_sem=core_send.at[link, slot % 2],
            recv_sem=core_recv.at[link, slot % 2],
            device_id={"partner": peer(0)},
            device_id_type=MESH,
        )

    def sign_copy(link):
        return pltpu.make_async_remote_copy(
            src_ref=signs,
            dst_ref=near_signs.at[link],
            send_sem=sign_send.at[link],
            recv_sem=sign_recv.at[link],
            device_id={"partner": peer(link + 1)},
            device_id_type=MESH,
        )

    def load_copy(chunk):
        return pltpu.make_async_copy(slab.at[chunk], held.at[chunk], load_sem.at[chunk])

    def out_copy(chunk):
        return pltpu.make_async_copy(held.at[chunk], out.at[chunk], out_sem.at[chunk])

    def combine(chunk, other, bit, scale):
        mine = side(bit) * scale
        step = min(rows, 64)

        @pl.loop(0, rows // step)
        def _(at):
            span = pl.ds(pl.multiple_of(at * step, step), step)
            held[chunk, span, :] = held[chunk, span, :] * mine + other[span, :] * scale

    for slot in range(depth):
        for link in range(links):
            copy = link_copy(link, slot)
            if copy is not None:
                copy.start()
    for chunk in range(slices):
        load_copy(chunk).start()
    signs[...] = jnp.broadcast_to(flips[...].astype(f32), signs.shape)
    for link in range(links):
        sign_copy(link).start()

    for link in range(links):
        sign_copy(link).wait()
    own_table = walsh_tile(tile)
    for link in range(links):
        for block in range(blocks):
            span = slice(block * tile, (block + 1) * tile)
            tables[link, 0, block] = (own_table * (signs[0:1, span] * side(link + 1))).astype(bf16)
            tables[link, 1, block] = (own_table * near_signs[link, 0:1, span]).astype(bf16)
    for chunk in range(slices):
        load_copy(chunk).wait()

    def transform(slot):
        count = min(links, slices - links * slot)
        width = min(cols, 256)
        tiles = cols // width

        @pl.loop(0, count * tiles)
        def _(at):
            link = at // tiles
            span = pl.ds(pl.multiple_of((at % tiles) * width, width), width)
            chunk = link + links * slot
            parts = []
            for block in range(blocks):
                lines = slice(block * tile, (block + 1) * tile)
                own_high, own_low = split_two(held[chunk, lines, span])
                far_high, far_low = split_two(landed[link, slot % slots, lines, span])
                own, far = tables[link, 0, block], tables[link, 1, block]
                sums = jnp.dot(own, own_high, preferred_element_type=f32)
                sums += jnp.dot(own, own_low, preferred_element_type=f32)
                sums += jnp.dot(far, far_high, preferred_element_type=f32)
                sums += jnp.dot(far, far_low, preferred_element_type=f32)
                parts.append(sums)
            for block, part in enumerate(butterflies(parts)):
                held[chunk, block * tile:(block + 1) * tile, span] = part

    def rows_of(blk):
        return pl.ds(pl.multiple_of(blk * share, share), share)

    def moment_copy(off):
        target = lax.rem(my_blk + off, blks)
        return pltpu.make_async_remote_copy(
            src_ref=moment.at[rows_of(target)],
            dst_ref=moment_in.at[off - 1],
            send_sem=moment_send.at[off - 1],
            recv_sem=moment_recv.at[off - 1],
            device_id={"blk": target},
            device_id_type=MESH,
        )

    def gram_copy(off):
        return pltpu.make_async_remote_copy(
            src_ref=gram,
            dst_ref=gram_in.at[off - 1],
            send_sem=gram_send.at[off - 1],
            recv_sem=gram_recv.at[off - 1],
            device_id={"blk": lax.rem(my_blk + off, blks)},
            device_id_type=MESH,
        )

    def pack_copy(bit):
        return pltpu.make_async_remote_copy(
            src_ref=packed.at[bit],
            dst_ref=packed_in.at[bit],
            send_sem=pack_send.at[bit],
            recv_sem=pack_recv.at[bit],
            device_id={"partner": peer(bit)},
            device_id_type=MESH,
        )

    def gather_copy(off):
        return pltpu.make_async_remote_copy(
            src_ref=packed.at[links + 1],
            dst_ref=gathered.at[off - 1],
            send_sem=gather_send.at[off - 1],
            recv_sem=gather_recv.at[off - 1],
            device_id={"blk": lax.rem(my_blk + off, blks)},
            device_id_type=MESH,
        )

    def contract_local():
        mode2[...] = mode2_wide[...].T
        moment_wide[...] = jnp.zeros_like(moment_wide)
        gram_wide[...] = jnp.zeros_like(gram_wide)
        samples = fibre_col.shape[1]

        @pl.loop(0, slices)
        def _(chunk):
            place = lax.broadcasted_iota(jnp.int32, (cols, samples), 0)
            sampled = (fibre_depth[...] - chunk) * cols + fibre_col[...]
            counts = jnp.sum((place == sampled).astype(f32), axis=1, keepdims=True)
            khatri = mode2[...] * mode3[pl.ds(chunk, 1), :]
            terms = split_three(khatri * counts)
            terms = [term.astype(f32) for term in terms]
            weights = jnp.concatenate(
                [
                    jnp.concatenate([terms[0], terms[1]], axis=1).astype(bf16),
                    jnp.concatenate([terms[2], jnp.zeros_like(terms[2])], axis=1).astype(bf16),
                ],
                axis=1,
            )
            turned = jnp.concatenate(split_three(khatri.T), axis=0)
            gram_wide[...] += jnp.dot(turned, weights, preferred_element_type=f32)

            @pl.loop(0, blocks)
            def _(block):
                lines = pl.ds(pl.multiple_of(block * tile, tile), tile)
                sums = moment_wide[lines, :]
                for term in split_three(held[chunk, lines, :]):
                    sums += jnp.dot(term, weights, preferred_element_type=f32)
                moment_wide[lines, :] = sums

        fold = gram_wide[:rank] + gram_wide[rank:2 * rank] + gram_wide[2 * rank:]
        gram[...] = fold[:, :rank] + fold[:, rank:2 * rank] + fold[:, 2 * rank:3 * rank]
        parts = []
        for block in range(blocks):
            value = moment_wide[block * tile:(block + 1) * tile, :]
            value = value[:, :rank] + value[:, rank:2 * rank] + value[:, 2 * rank:3 * rank]
            high, rest, low = split_three(value)
            table = tables[0, 0, block]
            sums = jnp.dot(table, low, preferred_element_type=f32)
            sums += jnp.dot(table, rest, preferred_element_type=f32)
            sums += jnp.dot(table, high, preferred_element_type=f32)
            parts.append(sums * side(1))
        for block, part in enumerate(butterflies(parts)):
            moment[block * tile:(block + 1) * tile, :] = part
        for off in range(1, blks):
            moment_copy(off).start()
            gram_copy(off).start()

    def solve_share():
        for off in range(1, blks):
            moment_copy(off).wait()
            gram_copy(off).wait()
        whole_gram = gram[...]
        own = moment[rows_of(my_blk), :]
        for off in range(1, blks):
            whole_gram = whole_gram + gram_in[off - 1]
            own = own + moment_in[off - 1]
        rows_idx = lax.broadcasted_iota(jnp.int32, (rank, rank), 0)
        cols_idx = lax.broadcasted_iota(jnp.int32, (rank, rank), 1)
        whole_gram = whole_gram * (1.0 / sample_count) + jnp.where(rows_idx == cols_idx, ridge, 0.0)
        solved = exact_dot(own * (scale / math.sqrt(sample_count)), inverse_of(whole_gram))
        packed[0] = jnp.concatenate([solved[: share // 2], solved[share // 2:]], axis=1)
        pack_copy(0).start()

    def pack_step(bit):
        pack_copy(bit).wait()
        packed[bit + 1] = packed[bit] * side(bit) + packed_in[bit]
        if bit < links:
            pack_copy(bit + 1).start()
        else:
            for off in range(1, blks):
                gather_copy(off).start()

    def write_share(blk, value):
        half = share // 2
        for at in range(2):
            lines = pl.ds(pl.multiple_of(blk * share + at * half, half), half)
            update[lines, :] = value[:, at * rank:(at + 1) * rank]

    def write_update():
        write_share(my_blk, packed[links + 1])
        for off in range(1, blks):
            gather_copy(off).wait()
            write_share(lax.rem(my_blk + blks - off, blks), gathered[off - 1])
        update_wide[...] = update[...].T

    contract_local()
    for slot in range(total):
        if 1 <= slot <= per_group:
            for link in range(links):
                copy = core_copy(link, slot - 1)
                if copy is not None:
                    copy.wait()
                    combine(chunk_at(link, slot - 1), core_landed.at[link, (slot - 1) % 2], 0, 1.0)
        if slot < per_group:
            for link in range(links):
                copy = link_copy(link, slot)
                if copy is not None:
                    copy.wait()
            transform(slot)
            for link in range(links):
                copy = core_copy(link, slot)
                if copy is not None:
                    copy.start()
        else:
            last = slot >= total - per_group
            for link in range(links):
                copy = link_copy(link, slot)
                if copy is not None:
                    copy.wait()
                    chunk = chunk_at(link, slot)
                    combine(chunk, landed.at[link, slot % slots], link + 1, scale if last else 1.0)
                    if last:
                        out_copy(chunk).start()
        if slot + depth < total:
            for link in range(links):
                copy = link_copy(link, slot + depth)
                if copy is not None:
                    copy.start()
        if slot == 1:
            solve_share()
        elif 2 <= slot <= links + 2:
            pack_step(slot - 2)
        elif slot == links + 3:
            write_update()
    for chunk in range(slices):
        out_copy(chunk).wait()


def shards(tensor_slab, sign_flips, mode2_factor, mode3_factor, fibre_col, fibre_depth):
    slices, rows, cols = tensor_slab.shape
    rank = mode2_factor.shape[1]
    parties, blks = lax.axis_size("partner"), lax.axis_size("blk")
    links = parties.bit_length() - 2
    per_group = -(-slices // links)
    depth = 2
    total = links * per_group
    slots = 4 if slices % links == 0 else total
    tile = min(256, rows)
    blocks = rows // tile
    share = rows // blks
    packed_shape = (share // 2, 2 * rank)
    others = max(blks - 1, 1)
    plan = (parties, blks, links, per_group, depth, slots)
    dma = pltpu.SemaphoreType.DMA
    vmem = pl.BlockSpec(memory_space=pltpu.VMEM)
    anywhere = pl.BlockSpec(memory_space=pl.ANY)
    mixed_slab, update_wide = pl.pallas_call(
        functools.partial(mixing_kernel, plan),
        out_shape=(
            jax.ShapeDtypeStruct(tensor_slab.shape, f32),
            jax.ShapeDtypeStruct((rank, rows), f32),
        ),
        in_specs=[anywhere, vmem, vmem, vmem, vmem, vmem],
        out_specs=(anywhere, vmem),
        scratch_shapes=[
            pltpu.VMEM((slices, rows, cols), f32),
            pltpu.VMEM((links, slots, rows, cols), f32),
            pltpu.VMEM((links, 2, rows, cols), f32),
            pltpu.VMEM((8, rows), f32),
            pltpu.VMEM((links, 8, rows), f32),
            pltpu.VMEM((links, 2, blocks, tile, tile), bf16),
            pltpu.VMEM((cols, rank), f32),
            pltpu.VMEM((rows, rank), f32),
            pltpu.VMEM((rows, 4 * rank), f32),
            pltpu.VMEM((3 * rank, 4 * rank), f32),
            pltpu.VMEM((rows, rank), f32),
            pltpu.VMEM((rank, rank), f32),
            pltpu.VMEM((others, share, rank), f32),
            pltpu.VMEM((others, rank, rank), f32),
            pltpu.VMEM((links + 2, *packed_shape), f32),
            pltpu.VMEM((links + 1, *packed_shape), f32),
            pltpu.VMEM((others, *packed_shape), f32),
            dma((slices,)),
            dma((links, slots)),
            dma((links, slots)),
            dma((links, 2)),
            dma((links, 2)),
            dma((links,)),
            dma((links,)),
            dma((slices,)),
            dma((others,)),
            dma((others,)),
            dma((others,)),
            dma((others,)),
            dma((links + 1,)),
            dma((links + 1,)),
            dma((others,)),
            dma((others,)),
        ],
        compiler_params=pltpu.CompilerParams(
            collective_id=0, has_side_effects=True, vmem_limit_bytes=56 * 2**20
        ),
    )(
        tensor_slab,
        sign_flips.reshape(1, rows),
        fibre_col.reshape(1, fibre_col.shape[0]),
        fibre_depth.reshape(1, fibre_depth.shape[0]),
        mode2_factor.T,
        mode3_factor,
    )
    return mixed_slab, update_wide.T


def solution(mesh):
    return jax.shard_map(
        shards,
        mesh=mesh,
        in_specs=(P(None, "partner", "blk"), P("partner"), P("blk", None), P(), P("blk"), P("blk")),
        out_specs=(P(None, "partner", "blk"), P("partner", None)),
        check_vma=False,
    )
```

```python
import functools
import math

import jax
import jax.numpy as jnp
from jax import lax
from jax.experimental import pallas as pl
from jax.experimental.pallas import tpu as pltpu
from jax.sharding import PartitionSpec as P

ridge = 0.1
MESH = pl.DeviceIdType.MESH
f32 = jnp.float32
bf16 = jnp.bfloat16


def walsh_tile(order):
    rows_idx = lax.broadcasted_iota(jnp.int32, (order, order), 0)
    cols_idx = lax.broadcasted_iota(jnp.int32, (order, order), 1)
    parity = jnp.bitwise_and(rows_idx, cols_idx)
    shift = order.bit_length() - 1
    while shift > 1:
        shift = (shift + 1) // 2
        parity = jnp.bitwise_xor(parity, jnp.right_shift(parity, shift))
    return (1 - 2 * jnp.bitwise_and(parity, 1)).astype(f32)


def butterflies(parts):
    stride = 1
    while stride < len(parts):
        parts = [
            parts[at] + parts[at + stride] if at & stride == 0 else parts[at - stride] - parts[at]
            for at in range(len(parts))
        ]
        stride *= 2
    return parts


def split_two(value):
    high = value.astype(bf16)
    return high, (value - high.astype(f32)).astype(bf16)


def exact_dot(left, right):
    return jnp.dot(left, right, precision=lax.Precision.HIGHEST, preferred_element_type=f32)


def eliminated(work, first, last):
    order = work.shape[0]
    rows_idx = lax.broadcasted_iota(jnp.int32, (order, order), 0)
    cols_idx = lax.broadcasted_iota(jnp.int32, (order, order), 1)

    def eliminate(at, work):
        on_row, on_col = rows_idx == at, cols_idx == at
        row = jnp.sum(jnp.where(on_row, work, 0.0), axis=0, keepdims=True)
        col = jnp.sum(jnp.where(on_col, work, 0.0), axis=1, keepdims=True)
        pivot = jnp.sum(jnp.where(on_col[0:1], row, 0.0), axis=1, keepdims=True)
        row = jnp.where(on_col[0:1], 1.0, row) / pivot
        return jnp.where(on_row, row, jnp.where(on_col, 0.0, work) - col * row)

    return lax.fori_loop(first, last, eliminate, work)


def identity_of(order):
    rows_idx = lax.broadcasted_iota(jnp.int32, (order, order), 0)
    cols_idx = lax.broadcasted_iota(jnp.int32, (order, order), 1)
    return (rows_idx == cols_idx).astype(f32)


def split_three(value):
    high, rest = split_two(value)
    low = (value - high.astype(f32) - rest.astype(f32)).astype(bf16)
    return high, rest, low


def mixing_kernel(plan, slab, flips, fibre_col, fibre_depth, mode2_wide, mode3, held, update_wide,
                  landed, core_landed, signs, near_signs, tables,
                  mode2, update, weights, moment_wide, gram_wide, moment, shares, shares_in,
                  gram, gram_in, solver, packed, packed_in, gathered,
                  load_sem, link_send, link_recv, core_send, core_recv, sign_send, sign_recv,
                  share_send, share_recv, gram_send, gram_recv, pack_send, pack_recv, gather_send, gather_recv):
    parties, blks, links, per_group, depth, slots = plan
    slices, rows, cols = held.shape
    tile = tables.shape[-1]
    blocks = rows // tile
    me = lax.axis_index("partner")
    my_blk = lax.axis_index("blk")
    share = rows // blks
    rank = mode2.shape[1]
    scale = 1.0 / math.sqrt(rows * parties)
    sample_count = fibre_col.shape[1] * blks

    def peer(bit):
        return jnp.bitwise_xor(me, 1 << bit)

    def side(bit):
        return (1 - 2 * jnp.bitwise_and(jnp.right_shift(me, bit), 1)).astype(f32)

    barrier = pltpu.get_barrier_semaphore()
    for bit in range(links + 1):
        pl.semaphore_signal(barrier, inc=1, device_id={"partner": peer(bit)}, device_id_type=MESH)
    for off in range(1, blks):
        pl.semaphore_signal(barrier, inc=1, device_id={"blk": lax.rem(my_blk + off, blks)}, device_id_type=MESH)
    pl.semaphore_wait(barrier, links + blks)

    total = links * per_group

    def chunk_at(link, slot):
        phase, turn = divmod(slot, per_group)
        chunk = (link - phase) % links + links * turn
        return chunk if chunk < slices else None

    def link_copy(link, slot):
        chunk = chunk_at(link, slot)
        if chunk is None:
            return None
        source = slab if slot < per_group else held
        return pltpu.make_async_remote_copy(
            src_ref=source.at[chunk],
            dst_ref=landed.at[link, slot % slots],
            send_sem=link_send.at[link, slot % slots],
            recv_sem=link_recv.at[link, slot % slots],
            device_id={"partner": peer(link + 1)},
            device_id_type=MESH,
        )

    def core_copy(link, slot):
        chunk = chunk_at(link, slot)
        if chunk is None:
            return None
        return pltpu.make_async_remote_copy(
            src_ref=held.at[chunk],
            dst_ref=core_landed.at[link, slot % 2],
            send_sem=core_send.at[link, slot % 2],
            recv_sem=core_recv.at[link, slot % 2],
            device_id={"partner": peer(0)},
            device_id_type=MESH,
        )

    def sign_copy(link):
        return pltpu.make_async_remote_copy(
            src_ref=signs,
            dst_ref=near_signs.at[link],
            send_sem=sign_send.at[link],
            recv_sem=sign_recv.at[link],
            device_id={"partner": peer(link + 1)},
            device_id_type=MESH,
        )

    def load_copy(chunk):
        return pltpu.make_async_copy(slab.at[chunk], held.at[chunk], load_sem.at[chunk])

    def combine(chunk, other, bit, scale):
        mine = side(bit) * scale
        step = min(rows, 64)

        @pl.loop(0, rows // step)
        def _(at):
            span = pl.ds(pl.multiple_of(at * step, step), step)
            held[chunk, span, :] = held[chunk, span, :] * mine + other[span, :] * scale

    for slot in range(depth):
        for link in range(links):
            copy = link_copy(link, slot)
            if copy is not None:
                copy.start()
    for chunk in range(slices):
        load_copy(chunk).start()
    signs[...] = jnp.broadcast_to(flips[...].astype(f32), signs.shape)
    for link in range(links):
        sign_copy(link).start()

    for link in range(links):
        sign_copy(link).wait()
    own_table = walsh_tile(tile)
    for link in range(links):
        for block in range(blocks):
            span = slice(block * tile, (block + 1) * tile)
            tables[link, 0, block] = (own_table * (signs[0:1, span] * side(link + 1))).astype(bf16)
            tables[link, 1, block] = (own_table * near_signs[link, 0:1, span]).astype(bf16)
    for chunk in range(slices):
        load_copy(chunk).wait()

    def transform(slot):
        count = min(links, slices - links * slot)
        width = min(cols, 256)
        tiles = cols // width

        @pl.loop(0, count * tiles)
        def _(at):
            link = at // tiles
            span = pl.ds(pl.multiple_of((at % tiles) * width, width), width)
            chunk = link + links * slot
            parts = []
            for block in range(blocks):
                lines = slice(block * tile, (block + 1) * tile)
                own_high, own_low = split_two(held[chunk, lines, span])
                far_high, far_low = split_two(landed[link, slot % slots, lines, span])
                own, far = tables[link, 0, block], tables[link, 1, block]
                sums = jnp.dot(own, own_high, preferred_element_type=f32)
                sums += jnp.dot(own, own_low, preferred_element_type=f32)
                sums += jnp.dot(far, far_high, preferred_element_type=f32)
                sums += jnp.dot(far, far_low, preferred_element_type=f32)
                parts.append(sums)
            for block, part in enumerate(butterflies(parts)):
                held[chunk, block * tile:(block + 1) * tile, span] = part

    def share_copy(off):
        target = lax.rem(my_blk + off, blks)
        return pltpu.make_async_remote_copy(
            src_ref=shares.at[target],
            dst_ref=shares_in.at[off - 1],
            send_sem=share_send.at[off - 1],
            recv_sem=share_recv.at[off - 1],
            device_id={"blk": target},
            device_id_type=MESH,
        )

    def gram_copy(off):
        return pltpu.make_async_remote_copy(
            src_ref=gram,
            dst_ref=gram_in.at[off - 1],
            send_sem=gram_send.at[off - 1],
            recv_sem=gram_recv.at[off - 1],
            device_id={"blk": lax.rem(my_blk + off, blks)},
            device_id_type=MESH,
        )

    def pack_copy(bit):
        return pltpu.make_async_remote_copy(
            src_ref=packed.at[bit],
            dst_ref=packed_in.at[bit],
            send_sem=pack_send.at[bit],
            recv_sem=pack_recv.at[bit],
            device_id={"partner": peer(bit)},
            device_id_type=MESH,
        )

    def gather_copy(off):
        return pltpu.make_async_remote_copy(
            src_ref=packed.at[links + 1],
            dst_ref=gathered.at[off - 1],
            send_sem=gather_send.at[off - 1],
            recv_sem=gather_recv.at[off - 1],
            device_id={"blk": lax.rem(my_blk + off, blks)},
            device_id_type=MESH,
        )

    def weigh_samples():
        mode2[...] = mode2_wide[...].T
        moment_wide[...] = jnp.zeros_like(moment_wide)
        gram_wide[...] = jnp.zeros_like(gram_wide)
        samples = fibre_col.shape[1]

        @pl.loop(0, slices)
        def _(chunk):
            place = lax.broadcasted_iota(jnp.int32, (cols, samples), 0)
            sampled = (fibre_depth[...] - chunk) * cols + fibre_col[...]
            counts = jnp.sum((place == sampled).astype(f32), axis=1, keepdims=True)
            khatri = mode2[...] * mode3[pl.ds(chunk, 1), :]
            terms = [term.astype(f32) for term in split_three(khatri * counts)]
            wide = jnp.concatenate(
                [
                    jnp.concatenate([terms[0], terms[1]], axis=1).astype(bf16),
                    jnp.concatenate([terms[2], jnp.zeros_like(terms[2])], axis=1).astype(bf16),
                ],
                axis=1,
            )
            weights[chunk] = wide
            turned = jnp.concatenate(split_three(khatri.T), axis=0)
            gram_wide[...] += jnp.dot(turned, wide, preferred_element_type=f32)

        fold = gram_wide[:rank] + gram_wide[rank:2 * rank] + gram_wide[2 * rank:]
        fold = fold[:, :rank] + fold[:, rank:2 * rank] + fold[:, 2 * rank:3 * rank]
        gram[...] = jnp.concatenate([fold, jnp.zeros_like(fold)], axis=1)
        for off in range(1, blks):
            gram_copy(off).start()

    def contract(slot):
        count = min(links, slices - links * slot)

        @pl.loop(0, count * blocks)
        def _(at):
            chunk = links * slot + at // blocks
            lines = pl.ds(pl.multiple_of((at % blocks) * tile, tile), tile)
            sums = moment_wide[lines, :]
            for term in split_three(held[chunk, lines, :]):
                sums += jnp.dot(term, weights[chunk], preferred_element_type=f32)
            moment_wide[lines, :] = sums

    def send_shares():
        parts = []
        for block in range(blocks):
            value = moment_wide[block * tile:(block + 1) * tile, :]
            value = value[:, :rank] + value[:, rank:2 * rank] + value[:, 2 * rank:3 * rank]
            high, rest, low = split_three(value)
            table = tables[0, 0, block]
            sums = jnp.dot(table, low, preferred_element_type=f32)
            sums += jnp.dot(table, rest, preferred_element_type=f32)
            sums += jnp.dot(table, high, preferred_element_type=f32)
            parts.append(sums * side(1))
        for block, part in enumerate(butterflies(parts)):
            moment[block * tile:(block + 1) * tile, :] = part
        half = share // 2
        for blk in range(blks):
            at = blk * share
            shares[blk] = jnp.concatenate([moment[at:at + half, :], moment[at + half:at + share, :]], axis=1)
        for off in range(1, blks):
            share_copy(off).start()

    def start_inverse():
        total_gram = gram[:, :rank]
        for off in range(1, blks):
            gram_copy(off).wait()
            total_gram = total_gram + gram_in[off - 1, :, :rank]
        total_gram = total_gram * (1.0 / sample_count) + identity_of(rank) * ridge
        solver[0] = total_gram
        solver[1] = eliminated(total_gram, 0, rank // 2)

    def finish_inverse():
        found = eliminated(solver[1], rank // 2, rank)
        solver[1] = found + exact_dot(found, identity_of(rank) - exact_dot(solver[0], found))

    def solve_share():
        own = shares[my_blk]
        for off in range(1, blks):
            share_copy(off).wait()
            own = own + shares_in[off - 1]
        own = own * (scale / math.sqrt(sample_count))
        packed[0] = jnp.concatenate(
            [exact_dot(own[:, :rank], solver[1]), exact_dot(own[:, rank:], solver[1])], axis=1
        )
        pack_copy(0).start()

    def pack_step(bit):
        pack_copy(bit).wait()
        packed[bit + 1] = packed[bit] * side(bit) + packed_in[bit]
        if bit < links:
            pack_copy(bit + 1).start()
        else:
            for off in range(1, blks):
                gather_copy(off).start()

    def write_share(blk, value):
        half = share // 2
        for at in range(2):
            lines = pl.ds(pl.multiple_of(blk * share + at * half, half), half)
            update[lines, :] = value[:, at * rank:(at + 1) * rank]

    def write_update():
        write_share(my_blk, packed[links + 1])
        for off in range(1, blks):
            gather_copy(off).wait()
            write_share(lax.rem(my_blk + blks - off, blks), gathered[off - 1])
        update_wide[...] = update[...].T

    weigh_samples()
    for slot in range(total):
        if 1 <= slot <= per_group:
            for link in range(links):
                copy = core_copy(link, slot - 1)
                if copy is not None:
                    copy.wait()
                    combine(chunk_at(link, slot - 1), core_landed.at[link, (slot - 1) % 2], 0, 1.0)
        if slot < per_group:
            contract(slot)
            if slot == per_group - 1:
                send_shares()
            for link in range(links):
                copy = link_copy(link, slot)
                if copy is not None:
                    copy.wait()
            transform(slot)
            for link in range(links):
                copy = core_copy(link, slot)
                if copy is not None:
                    copy.start()
        else:
            if slot == per_group:
                pack_step(0)
            if slot == total - 1:
                write_update()
            last = slot >= total - per_group
            for link in range(links):
                copy = link_copy(link, slot)
                if copy is not None:
                    copy.wait()
                    chunk = chunk_at(link, slot)
                    combine(chunk, landed.at[link, slot % slots], link + 1, scale if last else 1.0)
        if per_group < slot <= per_group + links:
            pack_step(slot - per_group)
        if slot + depth < total:
            for link in range(links):
                copy = link_copy(link, slot + depth)
                if copy is not None:
                    copy.start()
        if slot == 1:
            start_inverse()
        if slot == 2:
            finish_inverse()
        if slot == per_group - 1:
            solve_share()


def shards(tensor_slab, sign_flips, mode2_factor, mode3_factor, fibre_col, fibre_depth):
    slices, rows, cols = tensor_slab.shape
    rank = mode2_factor.shape[1]
    parties, blks = lax.axis_size("partner"), lax.axis_size("blk")
    links = parties.bit_length() - 2
    per_group = -(-slices // links)
    depth = 2
    total = links * per_group
    slots = 4 if slices % links == 0 else total
    tile = min(256, rows)
    blocks = rows // tile
    share = rows // blks
    packed_shape = (share // 2, 2 * rank)
    others = max(blks - 1, 1)
    plan = (parties, blks, links, per_group, depth, slots)
    dma = pltpu.SemaphoreType.DMA
    vmem = pl.BlockSpec(memory_space=pltpu.VMEM)
    anywhere = pl.BlockSpec(memory_space=pl.ANY)
    mixed_slab, update_wide = pl.pallas_call(
        functools.partial(mixing_kernel, plan),
        out_shape=(
            pltpu.VMEM(tensor_slab.shape, f32),
            jax.ShapeDtypeStruct((rank, rows), f32),
        ),
        in_specs=[anywhere, vmem, vmem, vmem, vmem, vmem],
        out_specs=(vmem, vmem),
        scratch_shapes=[
            pltpu.VMEM((links, slots, rows, cols), f32),
            pltpu.VMEM((links, 2, rows, cols), f32),
            pltpu.VMEM((8, rows), f32),
            pltpu.VMEM((links, 8, rows), f32),
            pltpu.VMEM((links, 2, blocks, tile, tile), bf16),
            pltpu.VMEM((cols, rank), f32),
            pltpu.VMEM((rows, rank), f32),
            pltpu.VMEM((slices, cols, 4 * rank), bf16),
            pltpu.VMEM((rows, 4 * rank), f32),
            pltpu.VMEM((3 * rank, 4 * rank), f32),
            pltpu.VMEM((rows, rank), f32),
            pltpu.VMEM((blks, *packed_shape), f32),
            pltpu.VMEM((others, *packed_shape), f32),
            pltpu.VMEM((rank, 2 * rank), f32),
            pltpu.VMEM((others, rank, 2 * rank), f32),
            pltpu.VMEM((2, rank, rank), f32),
            pltpu.VMEM((links + 2, *packed_shape), f32),
            pltpu.VMEM((links + 1, *packed_shape), f32),
            pltpu.VMEM((others, *packed_shape), f32),
            dma((slices,)),
            dma((links, slots)),
            dma((links, slots)),
            dma((links, 2)),
            dma((links, 2)),
            dma((links,)),
            dma((links,)),
            dma((others,)),
            dma((others,)),
            dma((others,)),
            dma((others,)),
            dma((links + 1,)),
            dma((links + 1,)),
            dma((others,)),
            dma((others,)),
        ],
        compiler_params=pltpu.CompilerParams(
            collective_id=0, has_side_effects=True, vmem_limit_bytes=40 * 2**20
        ),
    )(
        tensor_slab,
        sign_flips.reshape(1, rows),
        fibre_col.reshape(1, fibre_col.shape[0]),
        fibre_depth.reshape(1, fibre_depth.shape[0]),
        mode2_factor.T,
        mode3_factor,
    )
    return mixed_slab, update_wide.T


def solution(mesh):
    return jax.shard_map(
        shards,
        mesh=mesh,
        in_specs=(P(None, "partner", "blk"), P("partner"), P("blk", None), P(), P("blk"), P("blk")),
        out_specs=(P(None, "partner", "blk"), P("partner", None)),
        check_vma=False,
    )
```

```python
import functools
import math

import jax
import jax.numpy as jnp
from jax import lax
from jax.experimental import pallas as pl
from jax.experimental.pallas import tpu as pltpu
from jax.sharding import PartitionSpec as P

ridge = 0.1
MESH = pl.DeviceIdType.MESH
f32 = jnp.float32
bf16 = jnp.bfloat16


def walsh_tile(order):
    rows_idx = lax.broadcasted_iota(jnp.int32, (order, order), 0)
    cols_idx = lax.broadcasted_iota(jnp.int32, (order, order), 1)
    parity = jnp.bitwise_and(rows_idx, cols_idx)
    shift = order.bit_length() - 1
    while shift > 1:
        shift = (shift + 1) // 2
        parity = jnp.bitwise_xor(parity, jnp.right_shift(parity, shift))
    return (1 - 2 * jnp.bitwise_and(parity, 1)).astype(f32)


def butterflies(parts):
    stride = 1
    while stride < len(parts):
        parts = [
            parts[at] + parts[at + stride] if at & stride == 0 else parts[at - stride] - parts[at]
            for at in range(len(parts))
        ]
        stride *= 2
    return parts


def split_two(value):
    high = value.astype(bf16)
    return high, (value - high.astype(f32)).astype(bf16)


def exact_dot(left, right):
    return jnp.dot(left, right, precision=lax.Precision.HIGHEST, preferred_element_type=f32)


def eliminated(work, first, last):
    order = work.shape[0]
    rows_idx = lax.broadcasted_iota(jnp.int32, (order, order), 0)
    cols_idx = lax.broadcasted_iota(jnp.int32, (order, order), 1)

    def eliminate(at, work):
        on_row, on_col = rows_idx == at, cols_idx == at
        row = jnp.sum(jnp.where(on_row, work, 0.0), axis=0, keepdims=True)
        col = jnp.sum(jnp.where(on_col, work, 0.0), axis=1, keepdims=True)
        pivot = jnp.sum(jnp.where(on_col[0:1], row, 0.0), axis=1, keepdims=True)
        row = jnp.where(on_col[0:1], 1.0, row) / pivot
        return jnp.where(on_row, row, jnp.where(on_col, 0.0, work) - col * row)

    return lax.fori_loop(first, last, eliminate, work)


def identity_of(order):
    rows_idx = lax.broadcasted_iota(jnp.int32, (order, order), 0)
    cols_idx = lax.broadcasted_iota(jnp.int32, (order, order), 1)
    return (rows_idx == cols_idx).astype(f32)


def split_three(value):
    high, rest = split_two(value)
    low = (value - high.astype(f32) - rest.astype(f32)).astype(bf16)
    return high, rest, low


def mixing_kernel(plan, slab, flips, fibre_col, fibre_depth, mode2_wide, mode3, held, update_wide,
                  landed, core_landed, signs, near_signs, tables,
                  mode2, update, weights, moment_wide, gram_wide, moment, shares, shares_in,
                  gram, gram_in, solver, packed, packed_in, gathered,
                  load_sem, link_send, link_recv, core_send, core_recv, sign_send, sign_recv,
                  share_send, share_recv, gram_send, gram_recv, pack_send, pack_recv, gather_send, gather_recv):
    parties, blks, links, per_group, depth, slots = plan
    slices, rows, cols = held.shape
    tile = tables.shape[-1]
    blocks = rows // tile
    me = lax.axis_index("partner")
    my_blk = lax.axis_index("blk")
    share = rows // blks
    rank = mode2.shape[1]
    scale = 1.0 / math.sqrt(rows * parties)
    sample_count = fibre_col.shape[1] * blks

    def peer(bit):
        return jnp.bitwise_xor(me, 1 << bit)

    def side(bit):
        return (1 - 2 * jnp.bitwise_and(jnp.right_shift(me, bit), 1)).astype(f32)

    barrier = pltpu.get_barrier_semaphore()
    for bit in range(links + 1):
        pl.semaphore_signal(barrier, inc=1, device_id={"partner": peer(bit)}, device_id_type=MESH)
    for off in range(1, blks):
        pl.semaphore_signal(barrier, inc=1, device_id={"blk": lax.rem(my_blk + off, blks)}, device_id_type=MESH)
    pl.semaphore_wait(barrier, links + blks)

    total = links * per_group

    def chunk_at(link, slot):
        phase, turn = divmod(slot, per_group)
        chunk = (link - phase) % links + links * turn
        return chunk if chunk < slices else None

    def link_copy(link, slot):
        chunk = chunk_at(link, slot)
        if chunk is None:
            return None
        source = slab if slot < per_group else held
        return pltpu.make_async_remote_copy(
            src_ref=source.at[chunk],
            dst_ref=landed.at[link, slot % slots],
            send_sem=link_send.at[link, slot % slots],
            recv_sem=link_recv.at[link, slot % slots],
            device_id={"partner": peer(link + 1)},
            device_id_type=MESH,
        )

    def core_copy(link, slot):
        chunk = chunk_at(link, slot)
        if chunk is None:
            return None
        return pltpu.make_async_remote_copy(
            src_ref=held.at[chunk],
            dst_ref=core_landed.at[link, slot % 2],
            send_sem=core_send.at[link, slot % 2],
            recv_sem=core_recv.at[link, slot % 2],
            device_id={"partner": peer(0)},
            device_id_type=MESH,
        )

    def sign_copy(link):
        return pltpu.make_async_remote_copy(
            src_ref=signs,
            dst_ref=near_signs.at[link],
            send_sem=sign_send.at[link],
            recv_sem=sign_recv.at[link],
            device_id={"partner": peer(link + 1)},
            device_id_type=MESH,
        )

    def load_copy(chunk):
        return pltpu.make_async_copy(slab.at[chunk], held.at[chunk], load_sem.at[chunk])

    def combine(chunk, other, bit, scale):
        mine = side(bit) * scale
        step = min(rows, 64)

        @pl.loop(0, rows // step)
        def _(at):
            span = pl.ds(pl.multiple_of(at * step, step), step)
            held[chunk, span, :] = held[chunk, span, :] * mine + other[span, :] * scale

    for slot in range(depth):
        for link in range(links):
            copy = link_copy(link, slot)
            if copy is not None:
                copy.start()
    for chunk in range(slices):
        load_copy(chunk).start()
    signs[...] = jnp.broadcast_to(flips[...].astype(f32), signs.shape)
    for link in range(links):
        sign_copy(link).start()

    for link in range(links):
        sign_copy(link).wait()
    own_table = walsh_tile(tile)
    for link in range(links):
        for block in range(blocks):
            span = slice(block * tile, (block + 1) * tile)
            tables[link, 0, block] = (own_table * (signs[0:1, span] * side(link + 1))).astype(bf16)
            tables[link, 1, block] = (own_table * near_signs[link, 0:1, span]).astype(bf16)
    for chunk in range(slices):
        load_copy(chunk).wait()

    def transform(slot):
        count = min(links, slices - links * slot)
        width = min(cols, 256)
        tiles = cols // width

        @pl.loop(0, count * tiles)
        def _(at):
            link = at // tiles
            span = pl.ds(pl.multiple_of((at % tiles) * width, width), width)
            chunk = link + links * slot
            parts = []
            for block in range(blocks):
                lines = slice(block * tile, (block + 1) * tile)
                own_high, own_low = split_two(held[chunk, lines, span])
                far_high, far_low = split_two(landed[link, slot % slots, lines, span])
                own, far = tables[link, 0, block], tables[link, 1, block]
                sums = jnp.dot(own, own_high, preferred_element_type=f32)
                sums += jnp.dot(own, own_low, preferred_element_type=f32)
                sums += jnp.dot(far, far_high, preferred_element_type=f32)
                sums += jnp.dot(far, far_low, preferred_element_type=f32)
                parts.append(sums)
            for block, part in enumerate(butterflies(parts)):
                held[chunk, block * tile:(block + 1) * tile, span] = part

    def share_copy(off):
        target = lax.rem(my_blk + off, blks)
        return pltpu.make_async_remote_copy(
            src_ref=shares.at[target],
            dst_ref=shares_in.at[off - 1],
            send_sem=share_send.at[off - 1],
            recv_sem=share_recv.at[off - 1],
            device_id={"blk": target},
            device_id_type=MESH,
        )

    def gram_copy(off):
        return pltpu.make_async_remote_copy(
            src_ref=gram,
            dst_ref=gram_in.at[my_blk],
            send_sem=gram_send.at[off - 1],
            recv_sem=gram_recv.at[off - 1],
            device_id={"blk": lax.rem(my_blk + off, blks)},
            device_id_type=MESH,
        )

    def pack_copy(bit):
        return pltpu.make_async_remote_copy(
            src_ref=packed.at[bit],
            dst_ref=packed_in.at[bit],
            send_sem=pack_send.at[bit],
            recv_sem=pack_recv.at[bit],
            device_id={"partner": peer(bit)},
            device_id_type=MESH,
        )

    def gather_copy(off):
        return pltpu.make_async_remote_copy(
            src_ref=packed.at[links + 1],
            dst_ref=gathered.at[off - 1],
            send_sem=gather_send.at[off - 1],
            recv_sem=gather_recv.at[off - 1],
            device_id={"blk": lax.rem(my_blk + off, blks)},
            device_id_type=MESH,
        )

    def weigh_samples(slot):
        count = min(links, slices - links * slot)
        samples = fibre_col.shape[1]

        @pl.loop(0, count)
        def _(link):
            chunk = links * slot + link
            place = lax.broadcasted_iota(jnp.int32, (cols, samples), 0)
            sampled = (fibre_depth[...] - chunk) * cols + fibre_col[...]
            counts = jnp.sum((place == sampled).astype(f32), axis=1, keepdims=True)
            khatri = mode2[...] * mode3[pl.ds(chunk, 1), :]
            terms = [term.astype(f32) for term in split_three(khatri * counts)]
            wide = jnp.concatenate(
                [
                    jnp.concatenate([terms[0], terms[1]], axis=1).astype(bf16),
                    jnp.concatenate([terms[2], jnp.zeros_like(terms[2])], axis=1).astype(bf16),
                ],
                axis=1,
            )
            weights[link] = wide
            turned = jnp.concatenate(split_three(khatri.T), axis=0)
            gram_wide[...] += jnp.dot(turned, wide, preferred_element_type=f32)

    def send_gram():
        fold = gram_wide[:rank] + gram_wide[rank:2 * rank] + gram_wide[2 * rank:]
        fold = fold[:, :rank] + fold[:, rank:2 * rank] + fold[:, 2 * rank:3 * rank]
        gram[...] = jnp.concatenate([fold, jnp.zeros_like(fold)], axis=1)
        gram_in[my_blk] = gram[...]
        for off in range(1, blks):
            gram_copy(off).start()

    def contract(slot):
        count = min(links, slices - links * slot)

        @pl.loop(0, count * blocks)
        def _(at):
            link = at // blocks
            lines = pl.ds(pl.multiple_of((at % blocks) * tile, tile), tile)
            sums = moment_wide[lines, :]
            for term in split_three(held[links * slot + link, lines, :]):
                sums += jnp.dot(term, weights[link], preferred_element_type=f32)
            moment_wide[lines, :] = sums

    def send_shares():
        parts = []
        for block in range(blocks):
            value = moment_wide[block * tile:(block + 1) * tile, :]
            value = value[:, :rank] + value[:, rank:2 * rank] + value[:, 2 * rank:3 * rank]
            high, rest, low = split_three(value)
            table = tables[0, 0, block]
            sums = jnp.dot(table, low, preferred_element_type=f32)
            sums += jnp.dot(table, rest, preferred_element_type=f32)
            sums += jnp.dot(table, high, preferred_element_type=f32)
            parts.append(sums * side(1))
        for block, part in enumerate(butterflies(parts)):
            moment[block * tile:(block + 1) * tile, :] = part
        half = share // 2
        for blk in range(blks):
            at = blk * share
            shares[blk] = jnp.concatenate([moment[at:at + half, :], moment[at + half:at + share, :]], axis=1)
        for off in range(1, blks):
            share_copy(off).start()

    def start_inverse():
        for off in range(1, blks):
            gram_copy(off).wait()
        total_gram = gram_in[0, :, :rank]
        for blk in range(1, blks):
            total_gram = total_gram + gram_in[blk, :, :rank]
        total_gram = total_gram * (1.0 / sample_count) + identity_of(rank) * ridge
        solver[0] = total_gram
        solver[1] = eliminated(total_gram, 0, rank // 2)

    def finish_inverse():
        found = eliminated(solver[1], rank // 2, rank)
        solver[1] = found + exact_dot(found, identity_of(rank) - exact_dot(solver[0], found))

    def start_pack():
        own = shares[my_blk]
        for off in range(1, blks):
            share_copy(off).wait()
            own = own + shares_in[off - 1]
        packed[0] = own * (scale / math.sqrt(sample_count))
        pack_copy(0).start()

    def pack_step(bit):
        pack_copy(bit).wait()
        packed[bit + 1] = packed[bit] * side(bit) + packed_in[bit]
        if bit < links:
            pack_copy(bit + 1).start()
        else:
            for off in range(1, blks):
                gather_copy(off).start()

    def write_share(blk, value):
        half = share // 2
        for at in range(2):
            lines = pl.ds(pl.multiple_of(blk * share + at * half, half), half)
            update[lines, :] = value[:, at * rank:(at + 1) * rank]

    def write_update():
        write_share(my_blk, packed[links + 1])
        for off in range(1, blks):
            gather_copy(off).wait()
            write_share(lax.rem(my_blk + blks - off, blks), gathered[off - 1])
        step = min(rows, 256)
        for at in range(0, rows, step):
            update_wide[:, at:at + step] = exact_dot(update[at:at + step, :], solver[1]).T

    mode2[...] = mode2_wide[...].T
    moment_wide[...] = jnp.zeros_like(moment_wide)
    gram_wide[...] = jnp.zeros_like(gram_wide)
    for slot in range(total):
        if 1 <= slot <= per_group:
            for link in range(links):
                copy = core_copy(link, slot - 1)
                if copy is not None:
                    copy.wait()
                    combine(chunk_at(link, slot - 1), core_landed.at[link, (slot - 1) % 2], 0, 1.0)
        if slot < per_group:
            weigh_samples(slot)
            contract(slot)
            if slot == per_group - 1:
                send_gram()
                send_shares()
            for link in range(links):
                copy = link_copy(link, slot)
                if copy is not None:
                    copy.wait()
            transform(slot)
            for link in range(links):
                copy = core_copy(link, slot)
                if copy is not None:
                    copy.start()
        else:
            if slot == per_group:
                pack_step(0)
            if slot == total - 1:
                write_update()
            last = slot >= total - per_group
            for link in range(links):
                copy = link_copy(link, slot)
                if copy is not None:
                    copy.wait()
                    chunk = chunk_at(link, slot)
                    combine(chunk, landed.at[link, slot % slots], link + 1, scale if last else 1.0)
        if per_group < slot <= per_group + links:
            pack_step(slot - per_group)
        if slot + depth < total:
            for link in range(links):
                copy = link_copy(link, slot + depth)
                if copy is not None:
                    copy.start()
        if slot == per_group - 1:
            start_pack()
        if slot == per_group:
            start_inverse()
        if slot == per_group + 1:
            finish_inverse()


def shards(tensor_slab, sign_flips, mode2_factor, mode3_factor, fibre_col, fibre_depth):
    slices, rows, cols = tensor_slab.shape
    rank = mode2_factor.shape[1]
    parties, blks = lax.axis_size("partner"), lax.axis_size("blk")
    links = parties.bit_length() - 2
    per_group = -(-slices // links)
    depth = 2
    total = links * per_group
    slots = 4 if slices % links == 0 else total
    tile = min(256, rows)
    blocks = rows // tile
    share = rows // blks
    packed_shape = (share // 2, 2 * rank)
    others = max(blks - 1, 1)
    plan = (parties, blks, links, per_group, depth, slots)
    dma = pltpu.SemaphoreType.DMA
    vmem = pl.BlockSpec(memory_space=pltpu.VMEM)
    anywhere = pl.BlockSpec(memory_space=pl.ANY)
    mixed_slab, update_wide = pl.pallas_call(
        functools.partial(mixing_kernel, plan),
        out_shape=(
            pltpu.VMEM(tensor_slab.shape, f32),
            jax.ShapeDtypeStruct((rank, rows), f32),
        ),
        in_specs=[anywhere, vmem, vmem, vmem, vmem, vmem],
        out_specs=(vmem, vmem),
        scratch_shapes=[
            pltpu.VMEM((links, slots, rows, cols), f32),
            pltpu.VMEM((links, 2, rows, cols), f32),
            pltpu.VMEM((8, rows), f32),
            pltpu.VMEM((links, 8, rows), f32),
            pltpu.VMEM((links, 2, blocks, tile, tile), bf16),
            pltpu.VMEM((cols, rank), f32),
            pltpu.VMEM((rows, rank), f32),
            pltpu.VMEM((links, cols, 4 * rank), bf16),
            pltpu.VMEM((rows, 4 * rank), f32),
            pltpu.VMEM((3 * rank, 4 * rank), f32),
            pltpu.VMEM((rows, rank), f32),
            pltpu.VMEM((blks, *packed_shape), f32),
            pltpu.VMEM((others, *packed_shape), f32),
            pltpu.VMEM((rank, 2 * rank), f32),
            pltpu.VMEM((blks, rank, 2 * rank), f32),
            pltpu.VMEM((2, rank, rank), f32),
            pltpu.VMEM((links + 2, *packed_shape), f32),
            pltpu.VMEM((links + 1, *packed_shape), f32),
            pltpu.VMEM((others, *packed_shape), f32),
            dma((slices,)),
            dma((links, slots)),
            dma((links, slots)),
            dma((links, 2)),
            dma((links, 2)),
            dma((links,)),
            dma((links,)),
            dma((others,)),
            dma((others,)),
            dma((others,)),
            dma((others,)),
            dma((links + 1,)),
            dma((links + 1,)),
            dma((others,)),
            dma((others,)),
        ],
        compiler_params=pltpu.CompilerParams(
            collective_id=0, has_side_effects=True, vmem_limit_bytes=40 * 2**20
        ),
    )(
        tensor_slab,
        sign_flips.reshape(1, rows),
        fibre_col.reshape(1, fibre_col.shape[0]),
        fibre_depth.reshape(1, fibre_depth.shape[0]),
        mode2_factor.T,
        mode3_factor,
    )
    return mixed_slab, update_wide.T


def solution(mesh):
    return jax.shard_map(
        shards,
        mesh=mesh,
        in_specs=(P(None, "partner", "blk"), P("partner"), P("blk", None), P(), P("blk"), P("blk")),
        out_specs=(P(None, "partner", "blk"), P("partner", None)),
        check_vma=False,
    )
```

```python
import functools
import math

import jax
import jax.numpy as jnp
from jax import lax
from jax.experimental import pallas as pl
from jax.experimental.pallas import tpu as pltpu
from jax.sharding import PartitionSpec as P

ridge = 0.1
MESH = pl.DeviceIdType.MESH
f32 = jnp.float32
bf16 = jnp.bfloat16


def walsh_tile(order):
    rows_idx = lax.broadcasted_iota(jnp.int32, (order, order), 0)
    cols_idx = lax.broadcasted_iota(jnp.int32, (order, order), 1)
    parity = jnp.bitwise_and(rows_idx, cols_idx)
    shift = order.bit_length() - 1
    while shift > 1:
        shift = (shift + 1) // 2
        parity = jnp.bitwise_xor(parity, jnp.right_shift(parity, shift))
    return (1 - 2 * jnp.bitwise_and(parity, 1)).astype(f32)


def butterflies(parts):
    stride = 1
    while stride < len(parts):
        parts = [
            parts[at] + parts[at + stride] if at & stride == 0 else parts[at - stride] - parts[at]
            for at in range(len(parts))
        ]
        stride *= 2
    return parts


def split_two(value):
    high = value.astype(bf16)
    return high, (value - high.astype(f32)).astype(bf16)


def exact_dot(left, right):
    return jnp.dot(left, right, precision=lax.Precision.HIGHEST, preferred_element_type=f32)


def eliminated(work, first, last):
    order = work.shape[0]
    rows_idx = lax.broadcasted_iota(jnp.int32, (order, order), 0)
    cols_idx = lax.broadcasted_iota(jnp.int32, (order, order), 1)

    def eliminate(at, work):
        on_row, on_col = rows_idx == at, cols_idx == at
        row = jnp.sum(jnp.where(on_row, work, 0.0), axis=0, keepdims=True)
        col = jnp.sum(jnp.where(on_col, work, 0.0), axis=1, keepdims=True)
        pivot = jnp.sum(jnp.where(on_col[0:1], row, 0.0), axis=1, keepdims=True)
        row = jnp.where(on_col[0:1], 1.0, row) / pivot
        return jnp.where(on_row, row, jnp.where(on_col, 0.0, work) - col * row)

    return lax.fori_loop(first, last, eliminate, work)


def identity_of(order):
    rows_idx = lax.broadcasted_iota(jnp.int32, (order, order), 0)
    cols_idx = lax.broadcasted_iota(jnp.int32, (order, order), 1)
    return (rows_idx == cols_idx).astype(f32)


def split_three(value):
    high, rest = split_two(value)
    low = (value - high.astype(f32) - rest.astype(f32)).astype(bf16)
    return high, rest, low


def mixing_kernel(plan, slab, flips_far, col_far, depth_far, mode2_far, mode3_far, held, update_wide,
                  flips, fibre_col, fibre_depth, mode2_wide, mode3, fetch_sem, landed, core_landed, signs, near_signs, tables,
                  mode2, update, weights, moment_wide, gram_wide, moment, shares, shares_in,
                  gram, gram_in, solver, packed, packed_in, gathered,
                  load_sem, link_send, link_recv, core_send, core_recv, sign_send, sign_recv,
                  share_send, share_recv, gram_send, gram_recv, pack_send, pack_recv, gather_send, gather_recv):
    parties, blks, links, per_group, depth, slots = plan
    slices, rows, cols = held.shape
    tile = tables.shape[-1]
    blocks = rows // tile
    me = lax.axis_index("partner")
    my_blk = lax.axis_index("blk")
    share = rows // blks
    rank = mode2.shape[1]
    scale = 1.0 / math.sqrt(rows * parties)
    sample_count = fibre_col.shape[1] * blks

    def peer(bit):
        return jnp.bitwise_xor(me, 1 << bit)

    def side(bit):
        return (1 - 2 * jnp.bitwise_and(jnp.right_shift(me, bit), 1)).astype(f32)

    barrier = pltpu.get_barrier_semaphore()
    for bit in range(links + 1):
        pl.semaphore_signal(barrier, inc=1, device_id={"partner": peer(bit)}, device_id_type=MESH)
    for off in range(1, blks):
        pl.semaphore_signal(barrier, inc=1, device_id={"blk": lax.rem(my_blk + off, blks)}, device_id_type=MESH)
    pl.semaphore_wait(barrier, links + blks)

    total = links * per_group

    def chunk_at(link, slot):
        phase, turn = divmod(slot, per_group)
        chunk = (link - phase) % links + links * turn
        return chunk if chunk < slices else None

    def link_copy(link, slot):
        chunk = chunk_at(link, slot)
        if chunk is None:
            return None
        source = slab if slot < per_group else held
        return pltpu.make_async_remote_copy(
            src_ref=source.at[chunk],
            dst_ref=landed.at[link, slot % slots],
            send_sem=link_send.at[link, slot % slots],
            recv_sem=link_recv.at[link, slot % slots],
            device_id={"partner": peer(link + 1)},
            device_id_type=MESH,
        )

    def core_copy(link, slot):
        chunk = chunk_at(link, slot)
        if chunk is None:
            return None
        return pltpu.make_async_remote_copy(
            src_ref=held.at[chunk],
            dst_ref=core_landed.at[link, slot % 2],
            send_sem=core_send.at[link, slot % 2],
            recv_sem=core_recv.at[link, slot % 2],
            device_id={"partner": peer(0)},
            device_id_type=MESH,
        )

    def sign_copy(link):
        return pltpu.make_async_remote_copy(
            src_ref=signs,
            dst_ref=near_signs.at[link],
            send_sem=sign_send.at[link],
            recv_sem=sign_recv.at[link],
            device_id={"partner": peer(link + 1)},
            device_id_type=MESH,
        )

    def load_copy(chunk):
        return pltpu.make_async_copy(slab.at[chunk], held.at[chunk], load_sem.at[chunk])

    def combine(chunk, other, bit, scale):
        mine = side(bit) * scale
        step = min(rows, 64)

        @pl.loop(0, rows // step)
        def _(at):
            span = pl.ds(pl.multiple_of(at * step, step), step)
            held[chunk, span, :] = held[chunk, span, :] * mine + other[span, :] * scale

    for slot in range(depth):
        for link in range(links):
            copy = link_copy(link, slot)
            if copy is not None:
                copy.start()
    pairs = (
        (flips_far, flips),
        (col_far, fibre_col),
        (depth_far, fibre_depth),
        (mode2_far, mode2_wide),
        (mode3_far, mode3),
    )
    fetches = [pltpu.make_async_copy(far, near, fetch_sem.at[at]) for at, (far, near) in enumerate(pairs)]
    for copy in fetches:
        copy.start()
    for chunk in range(slices):
        load_copy(chunk).start()
    for copy in fetches:
        copy.wait()
    signs[...] = jnp.broadcast_to(flips[...].astype(f32), signs.shape)
    for link in range(links):
        sign_copy(link).start()

    for link in range(links):
        sign_copy(link).wait()
    own_table = walsh_tile(tile)
    for link in range(links):
        for block in range(blocks):
            span = slice(block * tile, (block + 1) * tile)
            tables[link, 0, block] = (own_table * (signs[0:1, span] * side(link + 1))).astype(bf16)
            tables[link, 1, block] = (own_table * near_signs[link, 0:1, span]).astype(bf16)
    for chunk in range(slices):
        load_copy(chunk).wait()

    def transform(slot):
        count = min(links, slices - links * slot)
        width = min(cols, 256)
        tiles = cols // width

        @pl.loop(0, count * tiles)
        def _(at):
            link = at // tiles
            span = pl.ds(pl.multiple_of((at % tiles) * width, width), width)
            chunk = link + links * slot
            parts = []
            for block in range(blocks):
                lines = slice(block * tile, (block + 1) * tile)
                own_high, own_low = split_two(held[chunk, lines, span])
                far_high, far_low = split_two(landed[link, slot % slots, lines, span])
                own, far = tables[link, 0, block], tables[link, 1, block]
                sums = jnp.dot(own, own_high, preferred_element_type=f32)
                sums += jnp.dot(own, own_low, preferred_element_type=f32)
                sums += jnp.dot(far, far_high, preferred_element_type=f32)
                sums += jnp.dot(far, far_low, preferred_element_type=f32)
                parts.append(sums)
            for block, part in enumerate(butterflies(parts)):
                held[chunk, block * tile:(block + 1) * tile, span] = part

    def share_copy(off):
        target = lax.rem(my_blk + off, blks)
        return pltpu.make_async_remote_copy(
            src_ref=shares.at[target],
            dst_ref=shares_in.at[off - 1],
            send_sem=share_send.at[off - 1],
            recv_sem=share_recv.at[off - 1],
            device_id={"blk": target},
            device_id_type=MESH,
        )

    def gram_copy(off):
        return pltpu.make_async_remote_copy(
            src_ref=gram,
            dst_ref=gram_in.at[my_blk],
            send_sem=gram_send.at[off - 1],
            recv_sem=gram_recv.at[off - 1],
            device_id={"blk": lax.rem(my_blk + off, blks)},
            device_id_type=MESH,
        )

    def pack_copy(bit):
        return pltpu.make_async_remote_copy(
            src_ref=packed.at[bit],
            dst_ref=packed_in.at[bit],
            send_sem=pack_send.at[bit],
            recv_sem=pack_recv.at[bit],
            device_id={"partner": peer(bit)},
            device_id_type=MESH,
        )

    def gather_copy(off):
        return pltpu.make_async_remote_copy(
            src_ref=packed.at[links + 1],
            dst_ref=gathered.at[off - 1],
            send_sem=gather_send.at[off - 1],
            recv_sem=gather_recv.at[off - 1],
            device_id={"blk": lax.rem(my_blk + off, blks)},
            device_id_type=MESH,
        )

    def weigh_samples(slot):
        count = min(links, slices - links * slot)
        samples = fibre_col.shape[1]

        @pl.loop(0, count)
        def _(link):
            chunk = links * slot + link
            place = lax.broadcasted_iota(jnp.int32, (cols, samples), 0)
            sampled = (fibre_depth[...] - chunk) * cols + fibre_col[...]
            counts = jnp.sum((place == sampled).astype(f32), axis=1, keepdims=True)
            khatri = mode2[...] * mode3[pl.ds(chunk, 1), :]
            terms = [term.astype(f32) for term in split_three(khatri * counts)]
            wide = jnp.concatenate(
                [
                    jnp.concatenate([terms[0], terms[1]], axis=1).astype(bf16),
                    jnp.concatenate([terms[2], jnp.zeros_like(terms[2])], axis=1).astype(bf16),
                ],
                axis=1,
            )
            weights[link] = wide
            turned = jnp.concatenate(split_three(khatri.T), axis=0)
            gram_wide[...] += jnp.dot(turned, wide, preferred_element_type=f32)

    def send_gram():
        fold = gram_wide[:rank] + gram_wide[rank:2 * rank] + gram_wide[2 * rank:]
        fold = fold[:, :rank] + fold[:, rank:2 * rank] + fold[:, 2 * rank:3 * rank]
        gram[...] = jnp.concatenate([fold, jnp.zeros_like(fold)], axis=1)
        gram_in[my_blk] = gram[...]
        for off in range(1, blks):
            gram_copy(off).start()

    def contract(slot):
        count = min(links, slices - links * slot)

        @pl.loop(0, count * blocks)
        def _(at):
            link = at // blocks
            lines = pl.ds(pl.multiple_of((at % blocks) * tile, tile), tile)
            sums = moment_wide[lines, :]
            for term in split_three(held[links * slot + link, lines, :]):
                sums += jnp.dot(term, weights[link], preferred_element_type=f32)
            moment_wide[lines, :] = sums

    def send_shares():
        parts = []
        for block in range(blocks):
            value = moment_wide[block * tile:(block + 1) * tile, :]
            value = value[:, :rank] + value[:, rank:2 * rank] + value[:, 2 * rank:3 * rank]
            high, rest, low = split_three(value)
            table = tables[0, 0, block]
            sums = jnp.dot(table, low, preferred_element_type=f32)
            sums += jnp.dot(table, rest, preferred_element_type=f32)
            sums += jnp.dot(table, high, preferred_element_type=f32)
            parts.append(sums * side(1))
        for block, part in enumerate(butterflies(parts)):
            moment[block * tile:(block + 1) * tile, :] = part
        half = share // 2
        for blk in range(blks):
            at = blk * share
            shares[blk] = jnp.concatenate([moment[at:at + half, :], moment[at + half:at + share, :]], axis=1)
        for off in range(1, blks):
            share_copy(off).start()

    def start_inverse():
        for off in range(1, blks):
            gram_copy(off).wait()
        total_gram = gram_in[0, :, :rank]
        for blk in range(1, blks):
            total_gram = total_gram + gram_in[blk, :, :rank]
        total_gram = total_gram * (1.0 / sample_count) + identity_of(rank) * ridge
        solver[0] = total_gram
        solver[1] = eliminated(total_gram, 0, rank // 2)

    def finish_inverse():
        found = eliminated(solver[1], rank // 2, rank)
        solver[1] = found + exact_dot(found, identity_of(rank) - exact_dot(solver[0], found))

    def start_pack():
        own = shares[my_blk]
        for off in range(1, blks):
            share_copy(off).wait()
            own = own + shares_in[off - 1]
        packed[0] = own * (scale / math.sqrt(sample_count))
        pack_copy(0).start()

    def pack_step(bit):
        pack_copy(bit).wait()
        packed[bit + 1] = packed[bit] * side(bit) + packed_in[bit]
        if bit < links:
            pack_copy(bit + 1).start()
        else:
            for off in range(1, blks):
                gather_copy(off).start()

    def write_share(blk, value):
        half = share // 2
        for at in range(2):
            lines = pl.ds(pl.multiple_of(blk * share + at * half, half), half)
            update[lines, :] = value[:, at * rank:(at + 1) * rank]

    def write_update():
        write_share(my_blk, packed[links + 1])
        for off in range(1, blks):
            gather_copy(off).wait()
            write_share(lax.rem(my_blk + blks - off, blks), gathered[off - 1])
        step = min(rows, 256)
        for at in range(0, rows, step):
            update_wide[:, at:at + step] = exact_dot(update[at:at + step, :], solver[1]).T

    mode2[...] = mode2_wide[...].T
    moment_wide[...] = jnp.zeros_like(moment_wide)
    gram_wide[...] = jnp.zeros_like(gram_wide)
    for slot in range(total):
        if 1 <= slot <= per_group:
            for link in range(links):
                copy = core_copy(link, slot - 1)
                if copy is not None:
                    copy.wait()
                    combine(chunk_at(link, slot - 1), core_landed.at[link, (slot - 1) % 2], 0, 1.0)
        if slot < per_group:
            weigh_samples(slot)
            contract(slot)
            if slot == per_group - 1:
                send_gram()
                send_shares()
            for link in range(links):
                copy = link_copy(link, slot)
                if copy is not None:
                    copy.wait()
            transform(slot)
            for link in range(links):
                copy = core_copy(link, slot)
                if copy is not None:
                    copy.start()
        else:
            if slot == per_group:
                pack_step(0)
            if slot == total - 1:
                write_update()
            last = slot >= total - per_group
            for link in range(links):
                copy = link_copy(link, slot)
                if copy is not None:
                    copy.wait()
                    chunk = chunk_at(link, slot)
                    combine(chunk, landed.at[link, slot % slots], link + 1, scale if last else 1.0)
        if per_group < slot <= per_group + links:
            pack_step(slot - per_group)
        if slot + depth < total:
            for link in range(links):
                copy = link_copy(link, slot + depth)
                if copy is not None:
                    copy.start()
        if slot == per_group - 1:
            start_pack()
        if slot == per_group:
            start_inverse()
        if slot == per_group + 1:
            finish_inverse()


def shards(tensor_slab, sign_flips, mode2_factor, mode3_factor, fibre_col, fibre_depth):
    slices, rows, cols = tensor_slab.shape
    rank = mode2_factor.shape[1]
    parties, blks = lax.axis_size("partner"), lax.axis_size("blk")
    links = parties.bit_length() - 2
    per_group = -(-slices // links)
    depth = 2
    total = links * per_group
    slots = 4 if slices % links == 0 else total
    tile = min(256, rows)
    blocks = rows // tile
    share = rows // blks
    packed_shape = (share // 2, 2 * rank)
    others = max(blks - 1, 1)
    plan = (parties, blks, links, per_group, depth, slots)
    dma = pltpu.SemaphoreType.DMA
    vmem = pl.BlockSpec(memory_space=pltpu.VMEM)
    anywhere = pl.BlockSpec(memory_space=pltpu.HBM)
    samples = fibre_col.shape[0]
    mixed_slab, update_wide = pl.pallas_call(
        functools.partial(mixing_kernel, plan),
        out_shape=(
            pltpu.VMEM(tensor_slab.shape, f32),
            pltpu.VMEM((rank, rows), f32),
        ),
        in_specs=[anywhere] * 6,
        out_specs=(vmem, vmem),
        scratch_shapes=[
            pltpu.VMEM((1, rows), jnp.int32),
            pltpu.VMEM((1, samples), jnp.int32),
            pltpu.VMEM((1, samples), jnp.int32),
            pltpu.VMEM((rank, cols), f32),
            pltpu.VMEM((slices, rank), f32),
            dma((5,)),
            pltpu.VMEM((links, slots, rows, cols), f32),
            pltpu.VMEM((links, 2, rows, cols), f32),
            pltpu.VMEM((8, rows), f32),
            pltpu.VMEM((links, 8, rows), f32),
            pltpu.VMEM((links, 2, blocks, tile, tile), bf16),
            pltpu.VMEM((cols, rank), f32),
            pltpu.VMEM((rows, rank), f32),
            pltpu.VMEM((links, cols, 4 * rank), bf16),
            pltpu.VMEM((rows, 4 * rank), f32),
            pltpu.VMEM((3 * rank, 4 * rank), f32),
            pltpu.VMEM((rows, rank), f32),
            pltpu.VMEM((blks, *packed_shape), f32),
            pltpu.VMEM((others, *packed_shape), f32),
            pltpu.VMEM((rank, 2 * rank), f32),
            pltpu.VMEM((blks, rank, 2 * rank), f32),
            pltpu.VMEM((2, rank, rank), f32),
            pltpu.VMEM((links + 2, *packed_shape), f32),
            pltpu.VMEM((links + 1, *packed_shape), f32),
            pltpu.VMEM((others, *packed_shape), f32),
            dma((slices,)),
            dma((links, slots)),
            dma((links, slots)),
            dma((links, 2)),
            dma((links, 2)),
            dma((links,)),
            dma((links,)),
            dma((others,)),
            dma((others,)),
            dma((others,)),
            dma((others,)),
            dma((links + 1,)),
            dma((links + 1,)),
            dma((others,)),
            dma((others,)),
        ],
        compiler_params=pltpu.CompilerParams(
            collective_id=0, has_side_effects=True, vmem_limit_bytes=40 * 2**20
        ),
    )(
        tensor_slab,
        sign_flips.reshape(1, rows),
        fibre_col.reshape(1, fibre_col.shape[0]),
        fibre_depth.reshape(1, fibre_depth.shape[0]),
        mode2_factor.T,
        mode3_factor,
    )
    return mixed_slab, update_wide.T


def solution(mesh):
    return jax.shard_map(
        shards,
        mesh=mesh,
        in_specs=(P(None, "partner", "blk"), P("partner"), P("blk", None), P(), P("blk"), P("blk")),
        out_specs=(P(None, "partner", "blk"), P("partner", None)),
        check_vma=False,
    )
```
